128 devices in a mesh: dp: 16 (over y_lo, x, core), ctx: 8 (over y_hi, z).
Axes of the slice: x: 4, y: 4 (y_hi: 2, y_lo: 2; y = y_hi * 2 + y_lo), z: 4, core: 2. Of those that a mesh axis runs over, the one named last changes fastest.
Arguments:
- tokens: bfloat16 [32, 1024, 4096], P('dp', 'ctx'), may hold values from -6 to 6
- queries: bfloat16 [32, 1024, 4096], P('dp', 'ctx'), may hold values from -6 to 6
- out_grad: bfloat16 [32, 1024, 4096], P('dp', 'ctx'), may hold values from -6 to 6
- kv_weight: bfloat16 [4096, 1024], replicated, may hold values from -0.09375 to 0.09375
- doc_lengths: int32 [32, 8], P('dp'), may hold values from 1 to 640, 1024 in all within a row
- swap_plan: int32 [16, 8, 3], P('dp', 'ctx'), may hold values from 0 to 1
Outputs:
- query_grad: bfloat16 [32, 1024, 4096], P('dp', 'ctx')
- weight_grad: float32 [4096, 1024], P(('dp', 'ctx'))
The draws below stay inside these ranges and needn't reach their ends.
Inputs may be any that keep to these rules, and one draw needn't show every extreme that they name: `doc_lengths`: each row sums to 1024; its longest document has exactly 640 tokens. `swap_plan`: entry r names, among the device's pages (sequence first, then page order), the one traded in round r.
All inputs are finite; a program needn't handle non-finite values.
Results may differ from the reference program's by a relative error of at most 0.014.
Values may be sent and summed in bfloat16 or wider, within the bound.
No kernel may reach another device: no remote copies, remote signals or barrier semaphores. Data moves between devices by JAX's collectives and lax.ppermute only.
A program may use at most 256 MiB of HBM per device.

```python
import math
import jax
import jax.numpy as jnp
import numpy as np
from jax import lax

D_IN = 4096
QHEADS = 32
KVHEADS = 4
HEAD = 128
PAGE = 128
ROUNDS = 3
DOCS = 8
SEQS = 2
TOK_DEV = 128
SEQ = 1024
BATCH = 32
MOST = 640
PAGES_DEV = 2
N_DP = 16
N_CTX = 8


def set_ends(array, stream_key, low, top_value):
    extent = array.shape
    index_at = [jax.random.randint(jax.random.fold_in(stream_key, axis), (), 0, extent[axis]) for axis in range(len(extent))]
    array = array.at[tuple(index_at)].set(low)
    longest = extent.index(max(extent))
    index_at[longest] = (index_at[longest] + 1) % extent[longest]
    return array.at[tuple(index_at)].set(top_value)


def shard_levels(stream_key, dims, shards, smallest, largest):
    loudness, own = 1.0, jax.random.fold_in(stream_key, 6)
    for axis_at, shards_of in shards:
        heights = jnp.exp(jax.random.uniform(jax.random.fold_in(own, axis_at), (shards_of,), jnp.float32, smallest / len(shards), largest / len(shards)))
        loudness = loudness * jnp.repeat(heights, dims[axis_at] // shards_of).reshape([-1 if axis == axis_at else 1 for axis in range(len(dims))])
    return loudness


def profile(number_of, total, reach, slope):
    portions = [(1 << 20) // math.isqrt(rank ** slope) + 1 for rank in range(2, number_of + 1)]
    surplus, counts = total - reach - (number_of - 1), [1] * (number_of - 1)
    while surplus > 0:
        movable = [i for i in range(number_of - 1) if counts[i] < reach]
        pool, remaining = sum([portions[i] for i in movable]), surplus
        for i in movable:
            extra = min(reach - counts[i], max(1, remaining * portions[i] // pool), surplus)
            counts[i] = counts[i] + extra
            surplus = surplus - extra
    return np.array([reach] + counts)


def uneven_parts(key, number_of, total, most, skew):
    if number_of == 2:
        one = jax.random.randint(key, (), max(1, total - most), min(most, total - 1) + 1)
        return jnp.stack([one, total - one])
    sizes = jnp.asarray(profile(number_of, total, most, skew), jnp.int32)
    twos = (number_of - 1) // 2
    giver, taker = sizes[1:1 + 2 * twos:2], sizes[2:2 + 2 * twos:2]
    margin = jnp.minimum(giver - 1, most - taker)
    shifted = jax.random.randint(jax.random.fold_in(key, 1), (twos,), 0, 1 << 20) % (margin + 1)
    sizes = sizes.at[1:1 + 2 * twos:2].set(giver - shifted).at[2:2 + 2 * twos:2].set(taker + shifted)
    return sizes[jax.random.permutation(jax.random.fold_in(key, 2), number_of)]


def normal_values(own_key, dims, scale, reach, shards=(), kind=jnp.bfloat16):
    result = scale * jax.random.normal(own_key, dims, jnp.float32)
    if shards:
        result = result * shard_levels(own_key, dims, shards, -0.22, 0.18)
    return jnp.clip(result, -reach, reach).astype(kind)


def setup_inputs(seed: int = 0) -> dict:
    key_list = jax.random.split(jax.random.key(seed), 7)
    tokens = normal_values(key_list[0], (BATCH, SEQ, D_IN), 1.0, 6.0, ((0, 16), (1, 8)))
    queries = normal_values(key_list[1], (BATCH, SEQ, QHEADS * HEAD), 1.0, 6.0, ((0, 16), (1, 8)))
    out_grad = normal_values(key_list[2], (BATCH, SEQ, QHEADS * HEAD), 1.0, 6.0, ((0, 16), (1, 8)))
    kv_weight = normal_values(key_list[3], (D_IN, 2 * KVHEADS * HEAD), D_IN ** -0.5, 0.09375)
    doc_lengths = jax.vmap(lambda own: uneven_parts(own, DOCS, SEQ, MOST, 2))(jax.random.split(key_list[4], BATCH)).reshape((BATCH, DOCS)).astype(jnp.int32)
    swap_plan = set_ends(jax.random.randint(key_list[5], (N_DP, N_CTX, ROUNDS), 0, PAGES_DEV), jax.random.fold_in(key_list[5], 1), 0, PAGES_DEV - 1).astype(jnp.int32)
    return {"tokens": tokens, "queries": queries, "out_grad": out_grad, "kv_weight": kv_weight, "doc_lengths": doc_lengths, "swap_plan": swap_plan}


def move_pages(arr, swap_plan):
    feat = arr.shape[-1]
    rows_per = TOK_DEV // PAGE
    pages = arr.reshape(N_DP, SEQS, N_CTX, rows_per, PAGE, feat).transpose(0, 2, 1, 3, 4, 5)
    pages = pages.reshape(N_DP, N_CTX, SEQS * rows_per, PAGE, feat)
    ranks = jnp.arange(N_DP, dtype=jnp.int32)
    slots = jnp.arange(SEQS * rows_per, dtype=jnp.int32)
    for step in range(ROUNDS):
        partner = jnp.bitwise_xor(ranks, 1 << step)
        select = swap_plan[:, :, step].astype(jnp.int32)
        other = pages[partner]
        incoming = jnp.take_along_axis(other, select[partner][:, :, None, None, None], axis=2)
        mask = (slots[None, None, :] == select[:, :, None])[:, :, :, None, None]
        pages = jnp.where(mask, incoming, pages)
    pages = pages.reshape(N_DP, N_CTX, SEQS, rows_per, PAGE, feat).transpose(0, 2, 1, 3, 4, 5)
    return pages.reshape(N_DP * SEQS, N_CTX * TOK_DEV, feat)


def block_sum(left, right):
    heads_per = QHEADS // KVHEADS
    left_blocks = left.reshape(heads_per, N_CTX, TOK_DEV, SEQ)
    right_blocks = right.reshape(N_CTX, TOK_DEV, heads_per, HEAD)
    parts = jnp.einsum('hctu,cthd->cud', left_blocks, right_blocks)
    parts = lax.optimization_barrier(parts.astype(jnp.bfloat16)).astype(jnp.float32)
    return jnp.sum(parts, axis=0)


def one_row(kv_weight, items):
    x_row, q_row, d_row, lengths = items
    scale = HEAD ** -0.5
    heads_per = QHEADS // KVHEADS
    kv_cols = KVHEADS * HEAD
    kv = jnp.dot(x_row, kv_weight, preferred_element_type=jnp.float32).astype(jnp.bfloat16)
    positions = jnp.arange(SEQ, dtype=jnp.int32)
    ends = jnp.cumsum(lengths.astype(jnp.int32))
    doc = jnp.sum((positions[:, None] >= ends[None, :]).astype(jnp.int32), axis=1)
    allowed = (doc[:, None] == doc[None, :]) & (positions[None, :] <= positions[:, None])
    dq_parts = []
    dk_parts = []
    dv_parts = []
    for group in range(KVHEADS):
        lo = group * heads_per * HEAD
        hi = lo + heads_per * HEAD
        q_group = q_row[:, lo:hi].reshape(SEQ, heads_per, HEAD).astype(jnp.float32)
        d_group = d_row[:, lo:hi].reshape(SEQ, heads_per, HEAD).astype(jnp.float32)
        k_group = kv[:, group * HEAD:(group + 1) * HEAD].astype(jnp.float32)
        v_group = kv[:, kv_cols + group * HEAD:kv_cols + (group + 1) * HEAD].astype(jnp.float32)
        scores = jnp.einsum('thd,ud->htu', q_group, k_group) * scale
        weights = jnp.where(allowed[None], jnp.exp(scores), 0.0)
        probs = weights / jnp.sum(weights, axis=-1, keepdims=True)
        probs_low = lax.optimization_barrier(probs.astype(jnp.bfloat16)).astype(jnp.float32)
        dprobs = jnp.einsum('thd,ud->htu', d_group, v_group)
        delta = jnp.sum(probs * dprobs, axis=-1, keepdims=True)
        dscores = (probs * (dprobs - delta) * scale).astype(jnp.bfloat16)
        dscores = lax.optimization_barrier(dscores).astype(jnp.float32)
        dq_group = jnp.einsum('htu,ud->thd', dscores, k_group)
        dq_parts.append(dq_group.reshape(SEQ, heads_per * HEAD).astype(jnp.bfloat16))
        dk_parts.append(block_sum(dscores, q_group))
        dv_parts.append(block_sum(probs_low, d_group))
    query_grad = jnp.concatenate(dq_parts, axis=1)
    kv_grad = jnp.concatenate(dk_parts + dv_parts, axis=1).astype(jnp.bfloat16)
    return query_grad, kv_grad


def reference(tokens, queries, out_grad, kv_weight, doc_lengths, swap_plan):
    moved_tokens = move_pages(tokens, swap_plan)
    moved_queries = move_pages(queries, swap_plan)
    moved_grad = move_pages(out_grad, swap_plan)
    query_grad, kv_grad = lax.map(partial_row(kv_weight), (moved_tokens, moved_queries, moved_grad, doc_lengths))
    flat_tokens = moved_tokens.reshape(-1, D_IN)
    flat_grad = kv_grad.reshape(-1, 2 * KVHEADS * HEAD)
    weight_grad = lax.dot_general(flat_tokens, flat_grad, (((0,), (0,)), ((), ())), preferred_element_type=jnp.float32)
    return query_grad, weight_grad


def partial_row(kv_weight):
    def apply_row(items):
        return one_row(kv_weight, items)
    return apply_row
```

```python
import functools

import jax
import jax.numpy as jnp
from jax import lax
from jax.experimental import pallas as pl
from jax.experimental.pallas import tpu as pltpu
from jax.sharding import PartitionSpec as P

HEAD = 128
ROUNDS = 3
AXES = ("dp", "ctx")
N_DP = 16
N_CTX = 8
TEAM = 8
WINDOW = 6
BLOCK = 128
GROUPS = 4
MASKED = -1e30
LOG2E = 1.4426950408889634


def move(value, target):
    route = []
    for dp in range(N_DP):
        for ctx in range(N_CTX):
            to_dp, to_ctx = target(dp, ctx)
            if 0 <= to_ctx < N_CTX:
                route.append((dp * N_CTX + ctx, to_dp * N_CTX + to_ctx))
    return lax.ppermute(value, AXES, route)


def flip_dp(bits):
    return lambda dp, ctx: (dp ^ bits, ctx)


def flip_ctx(bits):
    return lambda dp, ctx: (dp, ctx ^ bits)


def shift_ctx(by):
    return lambda dp, ctx: (dp, ctx + by)


def flip_y(low, high):
    return lambda dp, ctx: (dp ^ (low * 8), ctx ^ (high * 4))


def trade(pages, plan):
    for step in range(ROUNDS):
        outgoing = lax.dynamic_index_in_dim(pages, plan[step], 0, keepdims=False)
        incoming = move(outgoing, flip_dp(1 << step))
        mask = jnp.arange(2, dtype=jnp.int32) == plan[step]
        mask = mask.reshape((2,) + (1,) * (pages.ndim - 1))
        pages = jnp.where(mask, incoming[None], pages)
    return pages


def attention_kernel(
    first_ref, q_ref, d_ref, k_ref, v_ref, start_ref,
    dq_ref, part_ref,
    q_s, d_s, w_s, dp_s, acc_s,
):
    row = pl.program_id(0)
    first = first_ref[row]
    heads = q_ref.shape[-1] // HEAD
    queries = heads * BLOCK
    scale = HEAD ** (-0.5)
    for head in range(heads):
        at = slice(head * HEAD, (head + 1) * HEAD)
        q_s[head * BLOCK : (head + 1) * BLOCK, :] = q_ref[0, 0, :, at]
        d_s[head * BLOCK : (head + 1) * BLOCK, :] = d_ref[0, 0, :, at]
    start = start_ref[0]
    key_iota = lax.broadcasted_iota(jnp.int32, (BLOCK, BLOCK), 0)
    query_iota = lax.broadcasted_iota(jnp.int32, (BLOCK, BLOCK), 1) + (WINDOW - 1) * BLOCK
    nt = (((1,), (1,)), ((), ()))
    nn = (((1,), (0,)), ((), ()))

    def forward(index, carry):
        total, dot = carry
        at = pl.ds(pl.multiple_of(index * BLOCK, BLOCK), BLOCK)
        key_pos = key_iota + index * BLOCK
        seen = (key_pos >= start) & (key_pos <= query_iota)
        bias = jnp.where(seen, 0.0, MASKED)
        bias = jnp.concatenate([bias] * heads, axis=1)
        scores = lax.dot_general(k_ref[0, at, :], q_s[...], nt, preferred_element_type=jnp.float32)
        weights = jnp.exp2(scores * (scale * LOG2E) + bias)
        dprobs = lax.dot_general(v_ref[0, at, :], d_s[...], nt, preferred_element_type=jnp.float32)
        w_s[at, :] = weights
        dp_s[at, :] = dprobs
        total = total + jnp.sum(weights, axis=0, keepdims=True)
        dot = dot + jnp.sum(weights * dprobs, axis=0, keepdims=True)
        return total, dot

    zero = jnp.zeros((1, queries), jnp.float32)
    total, dot = lax.fori_loop(first, WINDOW, forward, (zero, zero))
    inverse = 1.0 / total
    delta = dot * inverse
    acc_s[...] = jnp.zeros_like(acc_s)

    def skip(index, carry):
        part_ref[index, 0] = jnp.zeros(part_ref.shape[2:], part_ref.dtype)
        return carry

    lax.fori_loop(0, first, skip, 0)

    def backward(index, carry):
        at = pl.ds(pl.multiple_of(index * BLOCK, BLOCK), BLOCK)
        probs = w_s[at, :] * inverse
        dscores = (probs * (dp_s[at, :] - delta) * scale).astype(jnp.bfloat16)
        dv = lax.dot_general(
            probs.astype(jnp.bfloat16), d_s[...], nn, preferred_element_type=jnp.float32
        )
        dk = lax.dot_general(dscores, q_s[...], nn, preferred_element_type=jnp.float32)
        part_ref[index, 0, :, :HEAD] = dk.astype(part_ref.dtype)
        part_ref[index, 0, :, HEAD:] = dv.astype(part_ref.dtype)
        acc_s[...] += lax.dot_general(
            k_ref[0, at, :], dscores, (((0,), (0,)), ((), ())), preferred_element_type=jnp.float32
        )
        return carry

    lax.fori_loop(first, WINDOW, backward, 0)
    for head in range(heads):
        at = slice(head * HEAD, (head + 1) * HEAD)
        dq_ref[0, :, at] = acc_s[:, head * BLOCK : (head + 1) * BLOCK].T.astype(dq_ref.dtype)


def attention(first, pages, window, start, group):
    rows, _, toks, width = pages.shape
    keys = window.shape[1]
    queries = width // HEAD * toks
    pairs = rows * queries * keys
    spec = pltpu.PrefetchScalarGridSpec(
        num_scalar_prefetch=1,
        grid=(rows,),
        in_specs=[
            pl.BlockSpec((1, 1, toks, width), lambda b, f: (b, 0, 0, 0)),
            pl.BlockSpec((1, 1, toks, width), lambda b, f: (b, 1, 0, 0)),
            pl.BlockSpec((1, keys, HEAD), lambda b, f: (b, 0, group)),
            pl.BlockSpec((1, keys, HEAD), lambda b, f: (b, 0, GROUPS + group)),
            pl.BlockSpec((1, 1, toks), lambda b, f: (b, 0, 0)),
        ],
        out_specs=[
            pl.BlockSpec((1, toks, width), lambda b, f: (b, 0, 0)),
            pl.BlockSpec((WINDOW, 1, BLOCK, 2 * HEAD), lambda b, f: (0, b, 0, 0)),
        ],
        scratch_shapes=[
            pltpu.VMEM((queries, HEAD), jnp.bfloat16),
            pltpu.VMEM((queries, HEAD), jnp.bfloat16),
            pltpu.VMEM((keys, queries), jnp.float32),
            pltpu.VMEM((keys, queries), jnp.float32),
            pltpu.VMEM((HEAD, queries), jnp.float32),
        ],
    )
    return pl.pallas_call(
        attention_kernel,
        grid_spec=spec,
        out_shape=[
            jax.ShapeDtypeStruct((rows, toks, width), jnp.bfloat16),
            jax.ShapeDtypeStruct((WINDOW, rows, BLOCK, 2 * HEAD), jnp.bfloat16),
        ],
        compiler_params=pltpu.CompilerParams(vmem_limit_bytes=32 * 1024 * 1024),
        cost_estimate=pl.CostEstimate(
            flops=10 * pairs * HEAD, bytes_accessed=8 * 1024 * 1024, transcendentals=pairs
        ),
    )(first, pages, pages, window, window, start)


def origins(plan_all, me):
    ranks = jnp.arange(TEAM, dtype=jnp.int32)
    table = ranks[:, None] * 2 + jnp.arange(2, dtype=jnp.int32)[None, :]
    for step in range(ROUNDS):
        select = plan_all[:, step]
        taken = jnp.where(select == 0, table[:, 0], table[:, 1])
        low = 1 << step
        swapped = jnp.flip(taken.reshape(TEAM // (2 * low), 2, low), axis=1).reshape(TEAM)
        table = jnp.where(
            jnp.arange(2, dtype=jnp.int32)[None, :] == select[:, None], swapped[:, None], table
        )
    return table


def per_device(tokens, queries, out_grad, kv_weight, doc_lengths, swap_plan):
    seqs, toks, width = tokens.shape
    pair = kv_weight.shape[1]
    cols = pair // 2
    group_width = queries.shape[2] // GROUPS
    dp = lax.axis_index("dp")
    ctx = lax.axis_index("ctx")
    team_rank = lax.rem(dp, TEAM)
    plan = swap_plan[0, 0]

    flat = tokens.reshape(seqs * toks, width)
    kv_own = jnp.dot(flat, kv_weight, preferred_element_type=jnp.float32).astype(jnp.bfloat16)
    kv_moved = trade(kv_own.reshape(seqs, toks, pair), plan)
    arrived = [move(kv_moved, shift_ctx(by)) for by in range(WINDOW - 1, 0, -1)]
    window = jnp.concatenate(arrived + [kv_moved], axis=1)

    ends = jnp.cumsum(doc_lengths, axis=1)
    pos = ctx * toks + jnp.arange(toks, dtype=jnp.int32)
    begun = jnp.max(
        jnp.where(ends[:, None, :] <= pos[None, :, None], ends[:, None, :], 0), axis=2
    )
    start = begun - (ctx - (WINDOW - 1)) * toks
    first = start[:, 0] // BLOCK
    start = start[:, None, :]

    moved = []
    for group in range(GROUPS):
        at = slice(group * group_width, (group + 1) * group_width)
        moved.append(trade(jnp.stack([queries[:, :, at], out_grad[:, :, at]], axis=1), plan))

    plans = plan[None]
    for step in range(ROUNDS):
        other = move(plans, flip_dp(1 << step))
        plans = jnp.concatenate([plans, other], axis=0)
    ranks = jnp.arange(TEAM, dtype=jnp.int32)
    plan_all = plans[ranks ^ team_rank]
    table = origins(plan_all, team_rank)
    part = width // (2 * TEAM)

    def columns(rank):
        return jnp.concatenate(
            [
                lax.dynamic_slice_in_dim(flat, rank * part, part, 1),
                lax.dynamic_slice_in_dim(flat, width // 2 + rank * part, part, 1),
            ],
            axis=1,
        )

    sources = [columns(team_rank)]
    sources += [move(columns(team_rank ^ bits), flip_dp(bits)) for bits in range(1, TEAM)]
    sources = jnp.stack(sources).reshape(TEAM * seqs, toks, 2 * part)
    ordered = []
    for bits in range(TEAM):
        for slot in range(seqs):
            origin = table[team_rank ^ bits, slot]
            place = ((origin // 2) ^ team_rank) * 2 + origin % 2
            ordered.append(lax.dynamic_index_in_dim(sources, place, 0, keepdims=False))
    ordered = jnp.concatenate(ordered, axis=0)

    z = lax.rem(ctx, 4)
    y_high = ctx // 4
    y_low = dp // TEAM
    query_parts = []
    grad_parts = []
    for group in range(GROUPS):
        query_grad, kv_part = attention(first, moved[group], window, start, group)
        query_parts.append(query_grad)
        total = kv_part[WINDOW - 1].astype(jnp.float32)
        for by in range(1, WINDOW):
            total = total + move(kv_part[WINDOW - 1 - by], shift_ctx(-by)).astype(jnp.float32)
        kv_grad = total.astype(jnp.bfloat16)
        chips = jnp.stack([kv_grad] + [move(kv_grad, flip_dp(2 * k)) for k in range(1, 4)])
        both = jnp.stack([chips, move(chips, flip_dp(1))], axis=1)
        both = both.reshape(TEAM * seqs * toks, 2 * HEAD)
        share = lax.dot_general(
            ordered, both, (((0,), (0,)), ((), ())), preferred_element_type=jnp.float32
        ).astype(jnp.bfloat16)
        share = share.reshape(2, 2, 4, -1, 2 * HEAD)
        kept = lax.dynamic_index_in_dim(share, z, 2, keepdims=False).astype(jnp.float32)
        for bits in range(1, 4):
            sent = lax.dynamic_index_in_dim(share, z ^ bits, 2, keepdims=False)
            kept = kept + move(sent, flip_ctx(bits)).astype(jnp.float32)

        def piece(low, high):
            value = lax.dynamic_index_in_dim(kept, y_low ^ low, 0, keepdims=False)
            return lax.dynamic_index_in_dim(value, y_high ^ high, 0, keepdims=False)

        final = piece(0, 0)
        for low, high in ((1, 0), (0, 1), (1, 1)):
            final = final + move(piece(low, high), flip_y(low, high))
        grad_parts.append(final)
    query_grad = jnp.concatenate(query_parts, axis=2)
    weight_grad = jnp.concatenate(
        [part[:, :HEAD] for part in grad_parts] + [part[:, HEAD:] for part in grad_parts], axis=1
    )
    return query_grad, weight_grad


def solution(mesh):
    in_specs = (
        P("dp", "ctx", None),
        P("dp", "ctx", None),
        P("dp", "ctx", None),
        P(),
        P("dp", None),
        P("dp", "ctx", None),
    )
    out_specs = (P("dp", "ctx", None), P(("dp", "ctx"), None))
    return jax.shard_map(
        per_device, mesh=mesh, in_specs=in_specs, out_specs=out_specs, check_vma=False
    )
```

```python
import functools

import jax
import jax.numpy as jnp
from jax import lax
from jax.experimental import pallas as pl
from jax.experimental.pallas import tpu as pltpu
from jax.sharding import PartitionSpec as P

HEAD = 128
ROUNDS = 3
AXES = ("dp", "ctx")
N_DP = 16
N_CTX = 8
TEAM = 8
WINDOW = 6
BLOCK = 128
GROUPS = 4
CHUNKS = 2
SHARE = GROUPS // CHUNKS
VMEM = 48 * 1024 * 1024
MASKED = -1e30
LOG2E = 1.4426950408889634
NT = (((1,), (1,)), ((), ()))
NN = (((1,), (0,)), ((), ()))
TN = (((0,), (0,)), ((), ()))


def move(value, target):
    route = []
    for dp in range(N_DP):
        for ctx in range(N_CTX):
            to_dp, to_ctx = target(dp, ctx)
            if 0 <= to_ctx < N_CTX:
                route.append((dp * N_CTX + ctx, to_dp * N_CTX + to_ctx))
    return lax.ppermute(value, AXES, route)


def flip_dp(bits):
    return lambda dp, ctx: (dp ^ bits, ctx)


def flip_ctx(bits):
    return lambda dp, ctx: (dp, ctx ^ bits)


def shift_ctx(by):
    return lambda dp, ctx: (dp, ctx + by)


def flip_y(low, high):
    return lambda dp, ctx: (dp ^ (low * 8), ctx ^ (high * 4))


ANYWHERE = pl.BlockSpec(memory_space=pl.ANY)


def light(read):
    return dict(
        compiler_params=pltpu.CompilerParams(vmem_limit_bytes=VMEM),
        cost_estimate=pl.CostEstimate(flops=0, bytes_accessed=read, transcendentals=0),
    )


def pick_kernel(step, count, plan_ref, *refs):
    came, kept = refs[:count], refs[count : 2 * count]
    send_ref, keep_ref = refs[-2:]
    same = plan_ref[step] == plan_ref[step - 1]

    def put(out, sources):
        for index, source in enumerate(sources):
            if count == 1:
                out[...] = source[...].reshape(out.shape)
            else:
                out[index] = source[...].reshape(out.shape[1:])

    @pl.when(same)
    def _():
        put(send_ref, came)
        put(keep_ref, kept)

    @pl.when(jnp.logical_not(same))
    def _():
        put(send_ref, kept)
        put(keep_ref, came)


def pick(step, plan, came, kept, chunk, chunks, held_back=()):
    toks, width = came[0].shape[-2:]
    width //= chunks
    steps = 1 if width <= 1024 else width // 1024
    block = width // steps
    first = chunk * steps
    in_specs = []
    for array in came:
        lead = array.shape[:-2]
        in_specs.append(
            pl.BlockSpec(lead + (toks, block), lambda g, p, n=len(lead): (0,) * n + (0, first + g))
        )
    for array in kept:
        if step == 1:
            in_specs.append(pl.BlockSpec((1, toks, block), lambda g, p: (1 - p[0], 0, first + g)))
        else:
            lead = array.shape[:-2]
            in_specs.append(
                pl.BlockSpec(
                    lead + (toks, block), lambda g, p, n=len(lead): (0,) * n + (0, first + g)
                )
            )
    lead = (len(came),) if len(came) > 1 else came[0].shape[:-2]
    shape = jax.ShapeDtypeStruct(lead + (toks, width), came[0].dtype)
    out = pl.BlockSpec(lead + (toks, block), lambda g, p, n=len(lead): (0,) * n + (0, g))
    return pl.pallas_call(
        functools.partial(pick_kernel, step, len(came)),
        grid_spec=pltpu.PrefetchScalarGridSpec(
            num_scalar_prefetch=1,
            grid=(steps,),
            in_specs=in_specs + [ANYWHERE] * len(held_back),
            out_specs=[out, out],
        ),
        out_shape=[shape, shape],
        **light(8 * 1024 * 1024),
    )(plan, *came, *kept, *held_back)


def rows_kernel(plan_ref, came_ref, kept_ref, *refs):
    out_ref = refs[-1]
    slot = plan_ref[ROUNDS - 1]
    out_ref[slot] = came_ref[...]
    out_ref[1 - slot] = kept_ref[...]


def rows_of(plan, came, kept, held_back=()):
    vmem = pl.BlockSpec(memory_space=pltpu.VMEM)
    return pl.pallas_call(
        rows_kernel,
        in_specs=[pl.BlockSpec(memory_space=pltpu.SMEM), vmem, vmem] + [ANYWHERE] * len(held_back),
        out_specs=vmem,
        out_shape=jax.ShapeDtypeStruct((2,) + came.shape, came.dtype),
        **light(1024 * 1024),
    )(plan, came, kept, *held_back)


def pages_kernel(count, plan_ref, *refs):
    for source, out in zip(refs[:count], refs[-count:]):
        out[...] = source[0]


def pages_of(plan, arrays, held_back=()):
    _, toks, width = arrays[0].shape
    block = min(width, 1024)
    shape = jax.ShapeDtypeStruct((toks, width), arrays[0].dtype)
    return pl.pallas_call(
        functools.partial(pages_kernel, len(arrays)),
        grid_spec=pltpu.PrefetchScalarGridSpec(
            num_scalar_prefetch=1,
            grid=(width // block,),
            in_specs=[pl.BlockSpec((1, toks, block), lambda g, p: (p[0], 0, g))] * len(arrays)
            + [ANYWHERE] * len(held_back),
            out_specs=[pl.BlockSpec((toks, block), lambda g, p: (0, g))] * len(arrays),
        ),
        out_shape=[shape] * len(arrays),
        **light(4 * 1024 * 1024),
    )(plan, *arrays, *held_back)


def sum_kernel(*refs):
    out_ref = refs[-1]
    half = out_ref.shape[-1] // 2
    for chunk in range(CHUNKS):
        parts = refs[chunk * WINDOW : (chunk + 1) * WINDOW]
        for group in range(SHARE):
            for kind in range(2):
                at = (group * 2 + kind) * HEAD
                to = kind * half + (chunk * SHARE + group) * HEAD
                total = parts[0][:, :, at : at + HEAD].astype(jnp.float32)
                for part in parts[1:]:
                    total = total + part[:, :, at : at + HEAD].astype(jnp.float32)
                out_ref[:, :, to : to + HEAD] = total.astype(out_ref.dtype)


def sum_of(chunks):
    vmem = pl.BlockSpec(memory_space=pltpu.VMEM)
    rows, toks, cols = chunks[0][0].shape
    return pl.pallas_call(
        sum_kernel,
        in_specs=[vmem] * (WINDOW * CHUNKS),
        out_specs=vmem,
        out_shape=jax.ShapeDtypeStruct((rows, toks, cols * CHUNKS), jnp.bfloat16),
        **light(4 * 1024 * 1024),
    )(*[part for parts in chunks for part in parts])


def columns_kernel(place_ref, *refs):
    sources = refs[: 2 * TEAM]
    outs = refs[-(TEAM // 2) :]
    part = sources[0].shape[1]
    for k, out in enumerate(outs):
        for side in range(2):
            for low in range(2):
                out[side, :, low * part : (low + 1) * part] = sources[(k * 2 + side) * 2 + low][...]


def columns_of(place, flat, held_back=()):
    rows, width = flat.shape
    part = width // (2 * TEAM)
    in_specs = []
    for k in range(TEAM // 2):
        for side in range(2):
            for low in range(2):
                in_specs.append(
                    pl.BlockSpec(
                        (rows, part),
                        lambda i, p, bits=2 * k + side, low=low: (0, low * TEAM + (p[0] ^ bits)),
                    )
                )
    shape = jax.ShapeDtypeStruct((2, rows, 2 * part), flat.dtype)
    out = pl.BlockSpec((2, rows, 2 * part), lambda i, p: (0, 0, 0))
    return pl.pallas_call(
        columns_kernel,
        grid_spec=pltpu.PrefetchScalarGridSpec(
            num_scalar_prefetch=1,
            grid=(1,),
            in_specs=in_specs + [ANYWHERE] * len(held_back),
            out_specs=[out] * (TEAM // 2),
        ),
        out_shape=[shape] * (TEAM // 2),
        **light(4 * 1024 * 1024),
    )(place, *([flat] * len(in_specs)), *held_back)


def attention_kernel(info_ref, *refs):
    q_ref, d_ref = refs[:2]
    k_refs = refs[2 : 2 + WINDOW]
    v_refs = refs[2 + WINDOW : 2 + 2 * WINDOW]
    start_ref = refs[2 + 2 * WINDOW]
    outs = len(refs) - 7 - WINDOW
    dq_ref = refs[outs]
    part_refs = refs[outs + 1 : outs + 1 + WINDOW]
    q_s, d_s, w_s, dp_s, acc_s, sum_s = refs[-6:]
    first = info_ref[1]
    heads = q_ref.shape[-1] // HEAD
    scale = HEAD ** (-0.5)
    for head in range(heads):
        at = slice(head * HEAD, (head + 1) * HEAD)
        q_s[head * BLOCK : (head + 1) * BLOCK, :] = q_ref[0, :, at]
        d_s[head * BLOCK : (head + 1) * BLOCK, :] = d_ref[0, :, at]
    start = start_ref[0]
    key_iota = lax.broadcasted_iota(jnp.int32, (BLOCK, BLOCK), 0)
    query_iota = lax.broadcasted_iota(jnp.int32, (BLOCK, BLOCK), 1) + (WINDOW - 1) * BLOCK
    sum_s[...] = jnp.zeros_like(sum_s)
    acc_s[...] = jnp.zeros_like(acc_s)

    for index in range(WINDOW):
        at = slice(index * BLOCK, (index + 1) * BLOCK)

        @pl.when(index >= first)
        def _():
            key_pos = key_iota + index * BLOCK
            seen = (key_pos >= start) & (key_pos <= query_iota)
            bias = jnp.concatenate([jnp.where(seen, 0.0, MASKED)] * heads, axis=1)
            scores = lax.dot_general(
                k_refs[index][0], q_s[...], NT, preferred_element_type=jnp.float32
            )
            weights = jnp.exp2(scores * (scale * LOG2E) + bias)
            dprobs = lax.dot_general(
                v_refs[index][0], d_s[...], NT, preferred_element_type=jnp.float32
            )
            w_s[at, :] = weights
            dp_s[at, :] = dprobs
            sum_s[0:1, :] += jnp.sum(weights, axis=0, keepdims=True)
            sum_s[1:2, :] += jnp.sum(weights * dprobs, axis=0, keepdims=True)

    inverse = 1.0 / sum_s[0:1, :]
    delta = sum_s[1:2, :] * inverse

    for index in range(WINDOW):
        at = slice(index * BLOCK, (index + 1) * BLOCK)

        @pl.when(index < first)
        def _():
            part_refs[index][0] = jnp.zeros(part_refs[index].shape[1:], jnp.bfloat16)

        @pl.when(index >= first)
        def _():
            probs = w_s[at, :] * inverse
            dscores = (probs * (dp_s[at, :] - delta) * scale).astype(jnp.bfloat16)
            dv = lax.dot_general(
                probs.astype(jnp.bfloat16), d_s[...], NN, preferred_element_type=jnp.float32
            )
            dk = lax.dot_general(dscores, q_s[...], NN, preferred_element_type=jnp.float32)
            part_refs[index][0, :, :HEAD] = dk.astype(jnp.bfloat16)
            part_refs[index][0, :, HEAD:] = dv.astype(jnp.bfloat16)
            acc_s[...] += lax.dot_general(
                k_refs[index][0], dscores, TN, preferred_element_type=jnp.float32
            )

    for head in range(heads):
        at = slice(head * HEAD, (head + 1) * HEAD)
        dq_ref[0, :, at] = acc_s[:, head * BLOCK : (head + 1) * BLOCK].T.astype(jnp.bfloat16)


def attention(info, page, blocks, start, chunk, dq, parts, held_back=()):
    _, toks, chunk_width = page.shape
    rows = start.shape[0]
    width = chunk_width // SHARE
    queries = width // HEAD * toks
    pairs = SHARE * queries * WINDOW * BLOCK
    in_specs = [
        pl.BlockSpec((1, toks, width), lambda g, f: (0, 0, g)),
        pl.BlockSpec((1, toks, width), lambda g, f: (1, 0, g)),
    ]
    in_specs += [pl.BlockSpec((1, BLOCK, HEAD), lambda g, f: (f[0], 0, chunk * SHARE + g))] * WINDOW
    in_specs += [
        pl.BlockSpec((1, BLOCK, HEAD), lambda g, f: (f[0], 0, GROUPS + chunk * SHARE + g))
    ] * WINDOW
    in_specs += [pl.BlockSpec((1, 1, toks), lambda g, f: (f[0], 0, 0))]
    args = [page, page] + list(blocks) + list(blocks) + [start]
    aliases = {}
    for place, array in enumerate([dq] + list(parts)):
        if array is not None:
            aliases[1 + len(args)] = place
            in_specs.append(ANYWHERE)
            args.append(array)
    in_specs += [ANYWHERE] * len(held_back)
    args += held_back
    part_shape = jax.ShapeDtypeStruct((rows, BLOCK, SHARE * 2 * HEAD), jnp.bfloat16)
    spec = pltpu.PrefetchScalarGridSpec(
        num_scalar_prefetch=1,
        grid=(SHARE,),
        in_specs=in_specs,
        out_specs=[pl.BlockSpec((1, toks, width), lambda g, f: (f[0], 0, chunk * SHARE + g))]
        + [pl.BlockSpec((1, BLOCK, 2 * HEAD), lambda g, f: (f[0], 0, g))] * WINDOW,
        scratch_shapes=[
            pltpu.VMEM((queries, HEAD), jnp.bfloat16),
            pltpu.VMEM((queries, HEAD), jnp.bfloat16),
            pltpu.VMEM((WINDOW * BLOCK, queries), jnp.float32),
            pltpu.VMEM((WINDOW * BLOCK, queries), jnp.float32),
            pltpu.VMEM((HEAD, queries), jnp.float32),
            pltpu.VMEM((8, queries), jnp.float32),
        ],
    )
    return pl.pallas_call(
        attention_kernel,
        grid_spec=spec,
        out_shape=[jax.ShapeDtypeStruct((rows, toks, GROUPS * width), jnp.bfloat16)]
        + [part_shape] * WINDOW,
        input_output_aliases=aliases,
        compiler_params=pltpu.CompilerParams(vmem_limit_bytes=VMEM),
        cost_estimate=pl.CostEstimate(
            flops=10 * pairs * HEAD, bytes_accessed=4 * 1024 * 1024, transcendentals=pairs
        ),
    )(info, *args)


def arrange_kernel(plan_ref, place_ref, *refs):
    sources, out_ref = refs[:-1], refs[-1]
    rank_me, z_me, low_me, high_me = (place_ref[i] for i in range(4))
    for rel, source in enumerate(sources):
        for page in range(2):
            rank = rank_me ^ rel
            slot = jnp.int32(page)
            for step in range(ROUNDS):
                to_rank = rank ^ (1 << step)
                goes = plan_ref[(rank ^ rank_me) * ROUNDS + step] == slot
                slot = jnp.where(goes, plan_ref[(to_rank ^ rank_me) * ROUNDS + step], slot)
                rank = jnp.where(goes, to_rank, rank)
            column = pl.multiple_of(((rank ^ rank_me) * 2 + slot) * BLOCK, BLOCK)
            data = source[page * BLOCK : (page + 1) * BLOCK, :].astype(jnp.float32)
            data = data.T.astype(jnp.bfloat16)
            for low in range(2):
                for high in range(2):
                    for z in range(4):
                        at = ((low * 2 + high) * 4 + z) * 32
                        to = (z ^ z_me) * 4 + (low ^ low_me) + (high ^ high_me) * 2
                        to = pl.multiple_of(to * 32, 32)
                        out_ref[pl.ds(to, 32), pl.ds(column, BLOCK)] = data[at : at + 32, :]


def arrange(plan_all, place, sources):
    rows, cols = sources[0].shape
    return pl.pallas_call(
        arrange_kernel,
        grid_spec=pltpu.PrefetchScalarGridSpec(
            num_scalar_prefetch=2,
            grid=(1,),
            in_specs=[pl.BlockSpec((rows, cols), lambda i, a, b: (0, 0))] * len(sources),
            out_specs=pl.BlockSpec((cols, rows * len(sources)), lambda i, a, b: (0, 0)),
        ),
        out_shape=jax.ShapeDtypeStruct((cols, rows * len(sources)), jnp.bfloat16),
        compiler_params=pltpu.CompilerParams(vmem_limit_bytes=VMEM),
        cost_estimate=pl.CostEstimate(flops=0, bytes_accessed=4 * 1024 * 1024, transcendentals=0),
    )(plan_all, place, *sources)


def product_kernel(x_ref, *refs):
    grads, outs = refs[:TEAM], refs[TEAM:]
    for z, out in enumerate(outs):
        rows = slice(z * 4 * 32, (z + 1) * 4 * 32)
        total = None
        for rel, grad in enumerate(grads):
            span = 2 * BLOCK
            block = jnp.concatenate([grad[0], grad[1]], axis=0)
            term = jnp.dot(
                x_ref[rows, rel * span : (rel + 1) * span],
                block,
                preferred_element_type=jnp.float32,
            )
            total = term if total is None else total + term
        out[...] = total.astype(out.dtype)


def product(x, grads):
    cols = grads[0].shape[-1]
    shape = (x.shape[0] // 4, cols)
    return pl.pallas_call(
        product_kernel,
        out_shape=[jax.ShapeDtypeStruct(shape, jnp.float32)]
        + [jax.ShapeDtypeStruct(shape, jnp.bfloat16)] * 3,
        compiler_params=pltpu.CompilerParams(vmem_limit_bytes=VMEM),
        cost_estimate=pl.CostEstimate(
            flops=2 * x.shape[0] * x.shape[1] * cols,
            bytes_accessed=5 * 1024 * 1024,
            transcendentals=0,
        ),
    )(x, *grads)


def per_device(tokens, queries, out_grad, kv_weight, doc_lengths, swap_plan):
    seqs, toks, width = tokens.shape
    pair = kv_weight.shape[1]
    cols = pair // 2
    group_width = queries.shape[2] // GROUPS
    dp = lax.axis_index("dp")
    ctx = lax.axis_index("ctx")
    rank = lax.rem(dp, TEAM)
    z = lax.rem(ctx, 4)
    y_high = ctx // 4
    y_low = dp // TEAM
    plan = swap_plan[0, 0]
    plans = jnp.stack([plan] + [move(plan, flip_dp(2 * k)) for k in range(1, TEAM // 2)])
    plan_all = jnp.stack([plans, move(plans, flip_dp(1))], axis=1).reshape(-1)

    ends = jnp.cumsum(doc_lengths, axis=1)
    pos = ctx * toks + jnp.arange(toks, dtype=jnp.int32)
    begun = jnp.max(
        jnp.where(ends[:, None, :] <= pos[None, :, None], ends[:, None, :], 0), axis=2
    )
    start = begun - (ctx - (WINDOW - 1)) * toks
    first = jnp.clip(start[:, 0] // BLOCK, 0, WINDOW - 1)
    start = start[:, None, :]
    row_came = plan[ROUNDS - 1]
    row_kept = 1 - row_came
    info_came = jnp.stack([row_came, jnp.where(row_came == 0, first[0], first[1])])
    info_kept = jnp.stack([row_kept, jnp.where(row_kept == 0, first[0], first[1])])

    def cross(step, value):
        return move(value, flip_dp(1 << step))

    halves = [queries, out_grad]
    flat = tokens.reshape(seqs * toks, width)
    kv = jnp.dot(flat, kv_weight, preferred_element_type=jnp.float32).astype(jnp.bfloat16)
    kv = kv.reshape(seqs, toks, pair)
    columns = columns_of(rank[None], flat)
    kv_came = cross(0, pages_of(plan, [kv], [plan_all, columns[0]])[0])
    there = {k: move(columns[k], flip_dp(2 * k)) for k in (1, 3)}
    there[0] = columns[0]
    loaded = [cross(0, one) for one in pages_of(plan, halves)]
    send, kv_kept = pick(1, plan, [kv_came], [kv], 0, 1)
    kv_came = cross(1, send)
    send, kv_kept = pick(2, plan, [kv_came], [kv_kept], 0, 1, [there[1], there[3]])
    kv_came = cross(2, send)
    send, kept = pick(1, plan, loaded, halves, 0, 1, [kv_came])
    came = cross(1, send)
    own = rows_of(plan, kv_came, kv_kept, [send])
    blocks = [move(own, shift_ctx(by)) for by in range(WINDOW - 1, 0, -1)] + [own]
    send_a, kept_a = pick(2, plan, [came], [kept], 0, CHUNKS, blocks[:4])
    came_a = cross(2, send_a)
    send_b, kept_b = pick(2, plan, [came], [kept], 1, CHUNKS, [send_a])
    came_b = cross(2, send_b)

    none = [None] * WINDOW

    def collect(parts):
        return parts[-1:] + [
            move(parts[WINDOW - 1 - by], shift_ctx(-by)) for by in range(1, WINDOW)
        ]

    dq, *parts = attention(info_kept, kept_a, blocks, start, 0, None, none)
    dq, *parts_a = attention(info_came, came_a, blocks, start, 0, dq, parts)
    dq, *parts = attention(info_kept, kept_b, blocks, start, 1, dq, none)
    parts_a = collect(parts_a)
    dq, *parts_b = attention(info_came, came_b, blocks, start, 1, dq, parts, parts_a[1:])
    late = columns_of(rank[None], flat, parts_b[:1])
    there[2] = move(late[2], flip_dp(4))
    grad = sum_of([parts_a, collect(parts_b)])

    sources = []
    for k in range(TEAM // 2):
        sources += [there[k][0], move(there[k][1], flip_dp(1))]
    place = jnp.stack([rank, z, y_low, y_high])
    arranged = arrange(plan_all, place, sources)
    grads = []
    for k in range(TEAM // 2):
        chip = move(grad, flip_dp(2 * k)) if k else grad
        grads += [chip, move(chip, flip_dp(1))]
    mine, *others = product(arranged, grads)
    for k, other in enumerate(others):
        mine = mine + move(other, flip_ctx(k + 1)).astype(jnp.float32)
    final = mine[:32]
    for k in range(1, 4):
        final = final + move(mine[32 * k : 32 * (k + 1)], flip_y(k % 2, k // 2))
    return dq, final


def solution(mesh):
    in_specs = (
        P("dp", "ctx", None),
        P("dp", "ctx", None),
        P("dp", "ctx", None),
        P(),
        P("dp", None),
        P("dp", "ctx", None),
    )
    out_specs = (P("dp", "ctx", None), P(("dp", "ctx"), None))
    return jax.shard_map(
        per_device, mesh=mesh, in_specs=in_specs, out_specs=out_specs, check_vma=False
    )
```

```python
import functools

import jax
import jax.numpy as jnp
from jax import lax
from jax.experimental import pallas as pl
from jax.experimental.pallas import tpu as pltpu
from jax.sharding import PartitionSpec as P

HEAD = 128
ROUNDS = 3
AXES = ("dp", "ctx")
N_DP = 16
N_CTX = 8
TEAM = 8
WINDOW = 6
BLOCK = 128
GROUPS = 4
CHUNKS = 2
SHARE = GROUPS // CHUNKS
VMEM = 48 * 1024 * 1024
MASKED = -1e30
LOG2E = 1.4426950408889634
NT = (((1,), (1,)), ((), ()))


def move(value, target):
    route = []
    for dp in range(N_DP):
        for ctx in range(N_CTX):
            to_dp, to_ctx = target(dp, ctx)
            if 0 <= to_ctx < N_CTX:
                route.append((dp * N_CTX + ctx, to_dp * N_CTX + to_ctx))
    return lax.ppermute(value, AXES, route)


def flip_dp(bits):
    return lambda dp, ctx: (dp ^ bits, ctx)


def flip_ctx(bits):
    return lambda dp, ctx: (dp, ctx ^ bits)


def shift_ctx(by):
    return lambda dp, ctx: (dp, ctx + by)


def shift_z(by, only=None, around=False):
    def target(dp, ctx):
        high, z = ctx // 4, ctx % 4
        if only is not None and (high, z) not in only:
            return dp, -1
        if not around and z + by > 3:
            return dp, -1
        return dp, high * 4 + (z + by) % 4

    return target


def lift(dp, ctx):
    return dp, ctx + 4


def flip_y(low, high):
    return lambda dp, ctx: (dp ^ (low * 8), ctx ^ (high * 4))


ANYWHERE = pl.BlockSpec(memory_space=pl.ANY)


def light(read):
    return dict(
        compiler_params=pltpu.CompilerParams(vmem_limit_bytes=VMEM),
        cost_estimate=pl.CostEstimate(flops=0, bytes_accessed=read, transcendentals=0),
    )


def copy_all(sems, pairs):
    copies = [
        pltpu.make_async_copy(source, target, sems.at[i])
        for i, (source, target) in enumerate(pairs)
    ]
    for copy in copies:
        copy.start()
    for copy in copies:
        copy.wait()


def copier(kernel, shapes, count, plan, *arrays):
    return pl.pallas_call(
        kernel,
        in_specs=[pl.BlockSpec(memory_space=pltpu.SMEM)] + [ANYWHERE] * len(arrays),
        out_specs=[pl.BlockSpec(memory_space=pltpu.VMEM)] * len(shapes),
        out_shape=[jax.ShapeDtypeStruct(shape, jnp.bfloat16) for shape in shapes],
        scratch_shapes=[pltpu.SemaphoreType.DMA((count,))],
        compiler_params=pltpu.CompilerParams(vmem_limit_bytes=VMEM),
        cost_estimate=pl.CostEstimate(flops=0, bytes_accessed=4 * 1024 * 1024, transcendentals=0),
    )(plan, *arrays)


def pages_of(plan, arrays, held_back=()):
    count = len(arrays)

    def kernel(plan_ref, *refs):
        outs, sems = refs[-1 - count : -1], refs[-1]
        copy_all(sems, [(ref.at[plan_ref[0]], out) for ref, out in zip(refs, outs)])

    return copier(kernel, [array.shape[1:] for array in arrays], count, plan, *arrays, *held_back)


def second_pages_of(plan, came, loaded, held_back=()):
    count = len(came)

    def kernel(plan_ref, *refs):
        out, sems = refs[-2], refs[-1]
        outs = [out.at[i] for i in range(count)]
        same = plan_ref[1] == plan_ref[0]

        @pl.when(same)
        def _():
            copy_all(sems, list(zip(refs[:count], outs)))

        @pl.when(jnp.logical_not(same))
        def _():
            others = [ref.at[1 - plan_ref[0]] for ref in refs[count : 2 * count]]
            copy_all(sems, list(zip(others, outs)))

    shape = (count,) + came[0].shape
    return copier(kernel, [shape], count, plan, *came, *loaded, *held_back)[0]


def third_pages_of(plan, came, came_before, loaded, part, parts, stays, held_back=()):
    count, toks, width = came.shape
    at = pl.ds(part * (width // parts), width // parts)
    whole = pl.ds(0, width)

    def kernel(plan_ref, came_ref, *refs):
        before, pages = refs[:count], refs[count : 2 * count]
        outs, sems = refs[-3 if stays else -2 : -1], refs[-1]
        first = plan_ref[1] == plan_ref[0]
        same = plan_ref[2] == plan_ref[1]

        def new(i, cols):
            return came_ref.at[i, :, cols]

        def old_from(came_first):
            def old(i, cols):
                if came_first:
                    return pages[i].at[1 - plan_ref[0], :, cols]
                return before[i].at[:, cols]

            return old

        for again in (True, False):
            for came_first in (True, False):

                @pl.when((same == again) & (first == came_first))
                def _():
                    old = old_from(came_first)
                    sources = (new, old) if again else (old, new)
                    pairs = [(sources[0](i, at), outs[0].at[i]) for i in range(count)]
                    if stays:
                        pairs += [(sources[1](i, whole), outs[1].at[i]) for i in range(count)]
                    copy_all(sems, pairs)

    shapes = [(count, toks, width // parts)] + [came.shape] * stays
    return copier(
        kernel, shapes, 2 * count, plan, came, *came_before, *loaded, *held_back
    )


def rows_of(plan, came, kept, held_back=()):
    def kernel(plan_ref, came_ref, kept_ref, *refs):
        out, sems = refs[-2:]
        slot = plan_ref[ROUNDS - 1]
        copy_all(sems, [(came_ref.at[0], out.at[slot]), (kept_ref.at[0], out.at[1 - slot])])

    return copier(kernel, [(2,) + came.shape[1:]], 2, plan, came, kept, *held_back)[0]


def sum_kernel(*refs):
    out_ref = refs[-1]
    half = out_ref.shape[-1] // 2
    for chunk in range(CHUNKS):
        parts = refs[chunk * WINDOW : (chunk + 1) * WINDOW]
        for group in range(SHARE):
            for kind in range(2):
                at = (group * 2 + kind) * HEAD
                to = kind * half + (chunk * SHARE + group) * HEAD
                total = parts[0][:, :, at : at + HEAD].astype(jnp.float32)
                for part in parts[1:]:
                    total = total + part[:, :, at : at + HEAD].astype(jnp.float32)
                out_ref[:, :, to : to + HEAD] = total.astype(out_ref.dtype)


def sum_of(chunks, held_back=()):
    vmem = pl.BlockSpec(memory_space=pltpu.VMEM)
    rows, toks, cols = chunks[0][0].shape
    return pl.pallas_call(
        sum_kernel,
        in_specs=[vmem] * (WINDOW * CHUNKS) + [ANYWHERE] * len(held_back),
        out_specs=vmem,
        out_shape=jax.ShapeDtypeStruct((rows, toks, cols * CHUNKS), jnp.bfloat16),
        **light(4 * 1024 * 1024),
    )(*[part for parts in chunks for part in parts], *held_back)


def columns_kernel(count, place_ref, *refs):
    sources, outs = refs[: 4 * count], refs[-count:]
    part = sources[0].shape[1]
    for k, out in enumerate(outs):
        for side in range(2):
            for low in range(2):
                out[side, :, low * part : (low + 1) * part] = sources[(k * 2 + side) * 2 + low][...]


def columns_of(place, flat, chips, held_back=()):
    rows, width = flat.shape
    part = width // (2 * TEAM)
    in_specs = []
    for k in chips:
        for side in range(2):
            for low in range(2):
                in_specs.append(
                    pl.BlockSpec(
                        (rows, part),
                        lambda i, p, bits=2 * k + side, low=low: (0, low * TEAM + (p[0] ^ bits)),
                    )
                )
    shape = jax.ShapeDtypeStruct((2, rows, 2 * part), flat.dtype)
    out = pl.BlockSpec((2, rows, 2 * part), lambda i, p: (0, 0, 0))
    return pl.pallas_call(
        functools.partial(columns_kernel, len(chips)),
        grid_spec=pltpu.PrefetchScalarGridSpec(
            num_scalar_prefetch=1,
            grid=(1,),
            in_specs=in_specs + [ANYWHERE] * len(held_back),
            out_specs=[out] * len(chips),
        ),
        out_shape=[shape] * len(chips),
        **light(1024 * 1024),
    )(place, *([flat] * len(in_specs)), *held_back)


def hold_kernel(*refs):
    pass


def hold(array, *held_back):
    return pl.pallas_call(
        hold_kernel,
        in_specs=[ANYWHERE] * (1 + len(held_back)),
        out_specs=ANYWHERE,
        out_shape=jax.ShapeDtypeStruct(array.shape, array.dtype),
        input_output_aliases={0: 0},
        **light(1024),
    )(array, *held_back)


def attention_kernel(info_ref, *refs):
    q_ref, d_ref = refs[:2]
    k_refs = refs[2 : 2 + WINDOW]
    v_refs = refs[2 + WINDOW : 2 + 2 * WINDOW]
    start_ref = refs[2 + 2 * WINDOW]
    outs = len(refs) - 7 - WINDOW
    dq_ref = refs[outs]
    part_refs = refs[outs + 1 : outs + 1 + WINDOW]
    q_s, d_s, w_s, dp_s, acc_s, sum_s = refs[-6:]
    first = info_ref[1]
    heads = q_ref.shape[-1] // HEAD
    scale = HEAD ** (-0.5)
    for head in range(heads):
        at = slice(head * HEAD, (head + 1) * HEAD)
        q_s[head * BLOCK : (head + 1) * BLOCK, :] = q_ref[0, :, at]
        d_s[head * BLOCK : (head + 1) * BLOCK, :] = d_ref[0, :, at]
    start = start_ref[0]
    key_iota = lax.broadcasted_iota(jnp.int32, (BLOCK, BLOCK), 0)
    query_iota = lax.broadcasted_iota(jnp.int32, (BLOCK, BLOCK), 1) + (WINDOW - 1) * BLOCK
    sum_s[...] = jnp.zeros_like(sum_s)
    acc_s[...] = jnp.zeros_like(acc_s)
    span = 2 * BLOCK
    spans = [slice(at, at + span) for at in range(0, heads * BLOCK, span)]

    def fold(array):
        return jnp.sum(array.reshape(BLOCK // 8, 8, span), axis=0)

    for index in range(WINDOW):
        at = slice(index * BLOCK, (index + 1) * BLOCK)

        @pl.when(index >= first)
        def _():
            key_pos = key_iota + index * BLOCK
            seen = (key_pos >= start) & (key_pos <= query_iota)
            bias = jnp.where(seen, 0.0, MASKED)
            bias = jnp.concatenate([bias, bias], axis=1)
            key = k_refs[index][0]
            value = v_refs[index][0]
            for cols in spans:
                scores = lax.dot_general(key, q_s[cols, :], NT, preferred_element_type=jnp.float32)
                dprobs = lax.dot_general(
                    value, d_s[cols, :], NT, preferred_element_type=jnp.float32
                )
                weights = jnp.exp2(scores * (scale * LOG2E) + bias)
                w_s[at, cols] = weights
                dp_s[at, cols] = dprobs
                sum_s[0:8, cols] += fold(weights)
                sum_s[8:16, cols] += fold(weights * dprobs)

    inverse = 1.0 / jnp.sum(sum_s[0:8, :], axis=0, keepdims=True)
    delta = jnp.sum(sum_s[8:16, :], axis=0, keepdims=True) * inverse

    for index in range(WINDOW):
        at = slice(index * BLOCK, (index + 1) * BLOCK)

        @pl.when(index < first)
        def _():
            part_refs[index][0] = jnp.zeros(part_refs[index].shape[1:], jnp.bfloat16)

        @pl.when(index >= first)
        def _():
            key = k_refs[index][0].astype(jnp.float32).T.astype(jnp.bfloat16)
            dk = jnp.zeros((BLOCK, HEAD), jnp.float32)
            dv = jnp.zeros((BLOCK, HEAD), jnp.float32)
            for cols in spans:
                probs = w_s[at, cols] * inverse[:, cols]
                dscores = (probs * (dp_s[at, cols] - delta[:, cols]) * scale).astype(jnp.bfloat16)
                dv += jnp.dot(
                    probs.astype(jnp.bfloat16), d_s[cols, :], preferred_element_type=jnp.float32
                )
                dk += jnp.dot(dscores, q_s[cols, :], preferred_element_type=jnp.float32)
                acc_s[:, cols] += jnp.dot(key, dscores, preferred_element_type=jnp.float32)
            part_refs[index][0, :, :HEAD] = dk.astype(jnp.bfloat16)
            part_refs[index][0, :, HEAD:] = dv.astype(jnp.bfloat16)

    for head in range(heads):
        at = slice(head * HEAD, (head + 1) * HEAD)
        dq_ref[0, :, at] = acc_s[:, head * BLOCK : (head + 1) * BLOCK].T.astype(jnp.bfloat16)


def attention(info, page, blocks, start, chunk, dq, parts, held_back=(), dq_width=4096):
    _, toks, page_width = page.shape
    rows = start.shape[0]
    width = dq_width // GROUPS
    first = chunk * SHARE if page_width == dq_width else 0
    queries = width // HEAD * toks
    pairs = SHARE * queries * WINDOW * BLOCK
    in_specs = [
        pl.BlockSpec((1, toks, width), lambda g, f: (0, 0, first + g)),
        pl.BlockSpec((1, toks, width), lambda g, f: (1, 0, first + g)),
    ]
    in_specs += [pl.BlockSpec((1, BLOCK, HEAD), lambda g, f: (f[0], 0, chunk * SHARE + g))] * WINDOW
    in_specs += [
        pl.BlockSpec((1, BLOCK, HEAD), lambda g, f: (f[0], 0, GROUPS + chunk * SHARE + g))
    ] * WINDOW
    in_specs += [pl.BlockSpec((1, 1, toks), lambda g, f: (f[0], 0, 0))]
    args = [page, page] + list(blocks) + list(blocks) + [start]
    aliases = {}
    for place, array in enumerate([dq] + list(parts)):
        if array is not None:
            aliases[1 + len(args)] = place
            in_specs.append(ANYWHERE)
            args.append(array)
    in_specs += [ANYWHERE] * len(held_back)
    args += held_back
    part_shape = jax.ShapeDtypeStruct((rows, BLOCK, SHARE * 2 * HEAD), jnp.bfloat16)
    spec = pltpu.PrefetchScalarGridSpec(
        num_scalar_prefetch=1,
        grid=(SHARE,),
        in_specs=in_specs,
        out_specs=[pl.BlockSpec((1, toks, width), lambda g, f: (f[0], 0, chunk * SHARE + g))]
        + [pl.BlockSpec((1, BLOCK, 2 * HEAD), lambda g, f: (f[0], 0, g))] * WINDOW,
        scratch_shapes=[
            pltpu.VMEM((queries, HEAD), jnp.bfloat16),
            pltpu.VMEM((queries, HEAD), jnp.bfloat16),
            pltpu.VMEM((WINDOW * BLOCK, queries), jnp.float32),
            pltpu.VMEM((WINDOW * BLOCK, queries), jnp.float32),
            pltpu.VMEM((HEAD, queries), jnp.float32),
            pltpu.VMEM((16, queries), jnp.float32),
        ],
    )
    return pl.pallas_call(
        attention_kernel,
        grid_spec=spec,
        out_shape=[jax.ShapeDtypeStruct((rows, toks, GROUPS * width), jnp.bfloat16)]
        + [part_shape] * WINDOW,
        input_output_aliases=aliases,
        compiler_params=pltpu.CompilerParams(vmem_limit_bytes=VMEM),
        cost_estimate=pl.CostEstimate(
            flops=10 * pairs * HEAD, bytes_accessed=4 * 1024 * 1024, transcendentals=pairs
        ),
    )(info, *args)


def arrange_kernel(plan_ref, place_ref, *refs):
    sources, out_ref = refs[:-1], refs[-1]
    rank_me, z_me, low_me, high_me = (place_ref[i] for i in range(4))
    for rel, source in enumerate(sources):
        for page in range(2):
            rank = rank_me ^ rel
            slot = jnp.int32(page)
            for step in range(ROUNDS):
                to_rank = rank ^ (1 << step)
                goes = plan_ref[(rank ^ rank_me) * ROUNDS + step] == slot
                slot = jnp.where(goes, plan_ref[(to_rank ^ rank_me) * ROUNDS + step], slot)
                rank = jnp.where(goes, to_rank, rank)
            column = pl.multiple_of(((rank ^ rank_me) * 2 + slot) * BLOCK, BLOCK)
            data = source[page * BLOCK : (page + 1) * BLOCK, :].astype(jnp.float32)
            data = data.T.astype(jnp.bfloat16)
            for low in range(2):
                for high in range(2):
                    for z in range(4):
                        at = ((low * 2 + high) * 4 + z) * 32
                        to = (z ^ z_me) * 4 + (low ^ low_me) + (high ^ high_me) * 2
                        to = pl.multiple_of(to * 32, 32)
                        out_ref[pl.ds(to, 32), pl.ds(column, BLOCK)] = data[at : at + 32, :]


def arrange(plan_all, place, sources):
    rows, cols = sources[0].shape
    return pl.pallas_call(
        arrange_kernel,
        grid_spec=pltpu.PrefetchScalarGridSpec(
            num_scalar_prefetch=2,
            grid=(1,),
            in_specs=[pl.BlockSpec((rows, cols), lambda i, a, b: (0, 0))] * len(sources),
            out_specs=pl.BlockSpec((cols, rows * len(sources)), lambda i, a, b: (0, 0)),
        ),
        out_shape=jax.ShapeDtypeStruct((cols, rows * len(sources)), jnp.bfloat16),
        compiler_params=pltpu.CompilerParams(vmem_limit_bytes=VMEM),
        cost_estimate=pl.CostEstimate(flops=0, bytes_accessed=4 * 1024 * 1024, transcendentals=0),
    )(plan_all, place, *sources)


def product_kernel(x_ref, *refs):
    grads, outs = refs[:TEAM], refs[TEAM:]
    for z, out in enumerate(outs):
        rows = slice(z * 4 * 32, (z + 1) * 4 * 32)
        total = None
        for rel, grad in enumerate(grads):
            span = 2 * BLOCK
            block = jnp.concatenate([grad[0], grad[1]], axis=0)
            term = jnp.dot(
                x_ref[rows, rel * span : (rel + 1) * span],
                block,
                preferred_element_type=jnp.float32,
            )
            total = term if total is None else total + term
        out[...] = total.astype(out.dtype)


def product(x, grads):
    cols = grads[0].shape[-1]
    shape = (x.shape[0] // 4, cols)
    return pl.pallas_call(
        product_kernel,
        out_shape=[jax.ShapeDtypeStruct(shape, jnp.float32)]
        + [jax.ShapeDtypeStruct(shape, jnp.bfloat16)] * 3,
        compiler_params=pltpu.CompilerParams(vmem_limit_bytes=VMEM),
        cost_estimate=pl.CostEstimate(
            flops=2 * x.shape[0] * x.shape[1] * cols,
            bytes_accessed=5 * 1024 * 1024,
            transcendentals=0,
        ),
    )(x, *grads)


def per_device(tokens, queries, out_grad, kv_weight, doc_lengths, swap_plan):
    seqs, toks, width = tokens.shape
    pair = kv_weight.shape[1]
    cols = pair // 2
    group_width = queries.shape[2] // GROUPS
    dp = lax.axis_index("dp")
    ctx = lax.axis_index("ctx")
    rank = lax.rem(dp, TEAM)
    z = lax.rem(ctx, 4)
    y_high = ctx // 4
    y_low = dp // TEAM
    plan = swap_plan[0, 0]
    plans = jnp.stack([plan] + [move(plan, flip_dp(2 * k)) for k in range(1, TEAM // 2)])
    plan_all = jnp.stack([plans, move(plans, flip_dp(1))], axis=1).reshape(-1)

    ends = jnp.cumsum(doc_lengths, axis=1)
    pos = ctx * toks + jnp.arange(toks, dtype=jnp.int32)
    begun = jnp.max(
        jnp.where(ends[:, None, :] <= pos[None, :, None], ends[:, None, :], 0), axis=2
    )
    start = begun - (ctx - (WINDOW - 1)) * toks
    first = jnp.clip(start[:, 0] // BLOCK, 0, WINDOW - 1)
    start = start[:, None, :]
    row_came = plan[ROUNDS - 1]
    row_kept = 1 - row_came
    info_came = jnp.stack([row_came, jnp.where(row_came == 0, first[0], first[1])])
    info_kept = jnp.stack([row_kept, jnp.where(row_kept == 0, first[0], first[1])])

    def cross(step, value):
        return move(value, flip_dp(1 << step))

    halves = [queries, out_grad]
    flat = tokens.reshape(seqs * toks, width)
    kv = jnp.dot(flat, kv_weight, preferred_element_type=jnp.float32).astype(jnp.bfloat16)
    kv = kv.reshape(seqs, toks, pair)
    kv_came = cross(0, pages_of(plan, [kv], [plan_all])[0])
    send = second_pages_of(plan, [kv_came], [kv])
    loaded = [cross(0, one) for one in pages_of(plan, halves, [send])]
    kv_second = cross(1, send)
    send, kv_kept = third_pages_of(plan, kv_second, [kv_came], [kv], 0, 1, True)
    kv_third = cross(2, send)
    send = second_pages_of(plan, loaded, halves)
    send = hold(send, kv_third)
    came = cross(1, send)
    own = rows_of(plan, kv_third, kv_kept, [send])
    near = [move(own, shift_z(by)) for by in (1, 2, 3)]
    above = move(own, lift)
    far = [
        move(above, shift_z(1, {(1, 0), (1, 1), (1, 2), (1, 3)}, True)),
        move(above, shift_z(2, {(1, 2), (1, 3)}, True)),
        move(above, shift_z(3, {(1, 1), (1, 2), (1, 3)}, True)),
    ]
    blocks = [
        far[0],
        above,
        near[2] + far[2],
        near[1] + far[1],
        jnp.where(z == 0, far[0], near[0]),
        own,
    ]
    send_a, kept = third_pages_of(
        plan, came, loaded, halves, 0, CHUNKS, True, held_back=near + far
    )
    came_a = cross(2, send_a)
    none = [None] * WINDOW

    def collect(parts):
        return parts[-1:] + [
            move(parts[WINDOW - 1 - by], shift_ctx(-by)) for by in range(1, WINDOW)
        ]

    there = [None] * (TEAM // 2)
    there[0], column = columns_of(rank[None], flat, [0, 2], [send_a])
    there[2] = move(column, flip_dp(4))
    dq, *parts_a = attention(info_kept, kept, blocks, start, 0, None, none)
    dq, *parts_b = attention(info_kept, kept, blocks, start, 1, dq, none)
    send_b = third_pages_of(
        plan, came, loaded, halves, 1, CHUNKS, False, held_back=[came_a, parts_b[0], there[2]]
    )[0]
    came_b = cross(2, send_b)
    dq, *parts_a = attention(info_came, came_a, blocks, start, 0, dq, parts_a)
    parts_a = collect(parts_a)
    columns = list(columns_of(rank[None], flat, [1, 3], [came_b]))
    for k, column in zip((1, 3), columns):
        there[k] = move(column, flip_dp(2 * k))
    dq, *parts_b = attention(
        info_came, came_b, blocks, start, 1, dq, parts_b, parts_a[1:4] + columns[:1]
    )
    grad = sum_of([parts_a, collect(parts_b)], [there[1], there[3]])

    sources = []
    for k in range(TEAM // 2):
        sources += [there[k][0], move(there[k][1], flip_dp(1))]
    place = jnp.stack([rank, z, y_low, y_high])
    arranged = arrange(plan_all, place, sources)
    grads = []
    for k in range(TEAM // 2):
        chip = move(grad, flip_dp(2 * k)) if k else grad
        grads += [chip, move(chip, flip_dp(1))]
    mine, *others = product(arranged, grads)
    for k, other in enumerate(others):
        mine = mine + move(other, flip_ctx(k + 1)).astype(jnp.float32)
    final = mine[:32]
    for k in range(1, 4):
        final = final + move(mine[32 * k : 32 * (k + 1)], flip_y(k % 2, k // 2))
    return dq, final


def solution(mesh):
    in_specs = (
        P("dp", "ctx", None),
        P("dp", "ctx", None),
        P("dp", "ctx", None),
        P(),
        P("dp", None),
        P("dp", "ctx", None),
    )
    out_specs = (P("dp", "ctx", None), P(("dp", "ctx"), None))
    return jax.shard_map(
        per_device, mesh=mesh, in_specs=in_specs, out_specs=out_specs, check_vma=False
    )
```

```python
import functools

import jax
import jax.numpy as jnp
from jax import lax
from jax.experimental import pallas as pl
from jax.experimental.pallas import tpu as pltpu
from jax.sharding import PartitionSpec as P

HEAD = 128
ROUNDS = 3
AXES = ("dp", "ctx")
N_DP = 16
N_CTX = 8
TEAM = 8
WINDOW = 6
BLOCK = 128
GROUPS = 4
CHUNKS = 2
SHARE = GROUPS // CHUNKS
VMEM = 48 * 1024 * 1024
MASKED = -1e30
JOIN = 6
LOG2E = 1.4426950408889634
NT = (((1,), (1,)), ((), ()))


def move(value, target):
    route = []
    for dp in range(N_DP):
        for ctx in range(N_CTX):
            to_dp, to_ctx = target(dp, ctx)
            if 0 <= to_ctx < N_CTX:
                route.append((dp * N_CTX + ctx, to_dp * N_CTX + to_ctx))
    return lax.ppermute(value, AXES, route)


def flip_dp(bits):
    return lambda dp, ctx: (dp ^ bits, ctx)


def flip_ctx(bits):
    return lambda dp, ctx: (dp, ctx ^ bits)


def shift_ctx(by):
    return lambda dp, ctx: (dp, ctx + by)


def shift_z(by, only=None, around=False):
    def target(dp, ctx):
        high, z = ctx // 4, ctx % 4
        if only is not None and (high, z) not in only:
            return dp, -1
        if not around and z + by > 3:
            return dp, -1
        return dp, high * 4 + (z + by) % 4

    return target


def lift(dp, ctx):
    return dp, ctx + 4


def flip_y(low, high):
    return lambda dp, ctx: (dp ^ (low * 8), ctx ^ (high * 4))


ANYWHERE = pl.BlockSpec(memory_space=pl.ANY)


def light(read):
    return dict(
        compiler_params=pltpu.CompilerParams(vmem_limit_bytes=VMEM),
        cost_estimate=pl.CostEstimate(flops=0, bytes_accessed=read, transcendentals=0),
    )


def copy_all(sems, pairs):
    copies = [
        pltpu.make_async_copy(source, target, sems.at[i])
        for i, (source, target) in enumerate(pairs)
    ]
    for copy in copies:
        copy.start()
    for copy in copies:
        copy.wait()


def copier(kernel, shapes, count, plan, *arrays):
    return pl.pallas_call(
        kernel,
        in_specs=[pl.BlockSpec(memory_space=pltpu.SMEM)] + [ANYWHERE] * len(arrays),
        out_specs=[pl.BlockSpec(memory_space=pltpu.VMEM)] * len(shapes),
        out_shape=[jax.ShapeDtypeStruct(shape, jnp.bfloat16) for shape in shapes],
        scratch_shapes=[pltpu.SemaphoreType.DMA((count,))],
        compiler_params=pltpu.CompilerParams(vmem_limit_bytes=VMEM),
        cost_estimate=pl.CostEstimate(flops=0, bytes_accessed=4 * 1024 * 1024, transcendentals=0),
    )(plan, *arrays)


def pages_of(plan, arrays, held_back=()):
    count = len(arrays)

    def kernel(plan_ref, *refs):
        outs, sems = refs[-1 - count : -1], refs[-1]
        copy_all(sems, [(ref.at[plan_ref[0]], out) for ref, out in zip(refs, outs)])

    return copier(kernel, [array.shape[1:] for array in arrays], count, plan, *arrays, *held_back)


def second_pages_of(plan, came, loaded, held_back=()):
    count = len(came)

    def kernel(plan_ref, *refs):
        out, sems = refs[-2], refs[-1]
        outs = [out.at[i] for i in range(count)]
        same = plan_ref[1] == plan_ref[0]

        @pl.when(same)
        def _():
            copy_all(sems, list(zip(refs[:count], outs)))

        @pl.when(jnp.logical_not(same))
        def _():
            others = [ref.at[1 - plan_ref[0]] for ref in refs[count : 2 * count]]
            copy_all(sems, list(zip(others, outs)))

    shape = (count,) + came[0].shape
    return copier(kernel, [shape], count, plan, *came, *loaded, *held_back)[0]


def third_pages_of(plan, came, came_before, loaded, part, parts, stays, held_back=()):
    count, toks, width = came.shape
    at = pl.ds(part * (width // parts), width // parts)
    whole = pl.ds(0, width)

    def kernel(plan_ref, came_ref, *refs):
        before, pages = refs[:count], refs[count : 2 * count]
        outs, sems = refs[-3 if stays else -2 : -1], refs[-1]
        first = plan_ref[1] == plan_ref[0]
        same = plan_ref[2] == plan_ref[1]

        def new(i, cols):
            return came_ref.at[i, :, cols]

        def old_from(came_first):
            def old(i, cols):
                if came_first:
                    return pages[i].at[1 - plan_ref[0], :, cols]
                return before[i].at[:, cols]

            return old

        for again in (True, False):
            for came_first in (True, False):

                @pl.when((same == again) & (first == came_first))
                def _():
                    old = old_from(came_first)
                    sources = (new, old) if again else (old, new)
                    pairs = [(sources[0](i, at), outs[0].at[i]) for i in range(count)]
                    if stays:
                        pairs += [(sources[1](i, whole), outs[1].at[i]) for i in range(count)]
                    copy_all(sems, pairs)

    shapes = [(count, toks, width // parts)] + [came.shape] * stays
    return copier(
        kernel, shapes, 2 * count, plan, came, *came_before, *loaded, *held_back
    )


def rows_of(plan, came, kept, held_back=()):
    def kernel(plan_ref, came_ref, kept_ref, *refs):
        out, sems = refs[-2:]
        slot = plan_ref[ROUNDS - 1]
        copy_all(sems, [(came_ref.at[0], out.at[slot]), (kept_ref.at[0], out.at[1 - slot])])

    return copier(kernel, [(2,) + came.shape[1:]], 2, plan, came, kept, *held_back)[0]


def sum_kernel(*refs):
    out_ref = refs[-1]
    half = out_ref.shape[-1] // 2
    for chunk in range(CHUNKS):
        parts = refs[chunk * WINDOW : (chunk + 1) * WINDOW]
        for group in range(SHARE):
            for kind in range(2):
                at = (group * 2 + kind) * HEAD
                to = kind * half + (chunk * SHARE + group) * HEAD
                total = parts[0][:, :, at : at + HEAD].astype(jnp.float32)
                for part in parts[1:]:
                    total = total + part[:, :, at : at + HEAD].astype(jnp.float32)
                out_ref[:, :, to : to + HEAD] = total.astype(out_ref.dtype)


def sum_of(chunks, held_back=()):
    vmem = pl.BlockSpec(memory_space=pltpu.VMEM)
    rows, toks, cols = chunks[0][0].shape
    return pl.pallas_call(
        sum_kernel,
        in_specs=[vmem] * (WINDOW * CHUNKS) + [ANYWHERE] * len(held_back),
        out_specs=vmem,
        out_shape=jax.ShapeDtypeStruct((rows, toks, cols * CHUNKS), jnp.bfloat16),
        **light(4 * 1024 * 1024),
    )(*[part for parts in chunks for part in parts], *held_back)


def columns_kernel(count, place_ref, *refs):
    sources, outs = refs[: 4 * count], refs[-count:]
    part = sources[0].shape[1]
    for k, out in enumerate(outs):
        for side in range(2):
            for low in range(2):
                out[side, :, low * part : (low + 1) * part] = sources[(k * 2 + side) * 2 + low][...]


def columns_of(place, flat, chips, held_back=()):
    rows, width = flat.shape
    part = width // (2 * TEAM)
    in_specs = []
    for k in chips:
        for side in range(2):
            for low in range(2):
                in_specs.append(
                    pl.BlockSpec(
                        (rows, part),
                        lambda i, p, bits=2 * k + side, low=low: (0, low * TEAM + (p[0] ^ bits)),
                    )
                )
    shape = jax.ShapeDtypeStruct((2, rows, 2 * part), flat.dtype)
    out = pl.BlockSpec((2, rows, 2 * part), lambda i, p: (0, 0, 0))
    return pl.pallas_call(
        functools.partial(columns_kernel, len(chips)),
        grid_spec=pltpu.PrefetchScalarGridSpec(
            num_scalar_prefetch=1,
            grid=(1,),
            in_specs=in_specs + [ANYWHERE] * len(held_back),
            out_specs=[out] * len(chips),
        ),
        out_shape=[shape] * len(chips),
        **light(1024 * 1024),
    )(place, *([flat] * len(in_specs)), *held_back)


def hold_kernel(*refs):
    pass


def hold(array, *held_back):
    return pl.pallas_call(
        hold_kernel,
        in_specs=[ANYWHERE] * (1 + len(held_back)),
        out_specs=ANYWHERE,
        out_shape=jax.ShapeDtypeStruct(array.shape, array.dtype),
        input_output_aliases={0: 0},
        **light(1024),
    )(array, *held_back)


def attention_kernel(info_ref, *refs):
    q_ref, d_ref = refs[:2]
    k_refs = refs[2 : 2 + WINDOW]
    v_refs = refs[2 + WINDOW : 2 + 2 * WINDOW]
    start_ref = refs[2 + 2 * WINDOW]
    outs = len(refs) - 7 - WINDOW
    dq_ref = refs[outs]
    part_refs = refs[outs + 1 : outs + 1 + WINDOW]
    q_s, d_s, w_s, dp_s, acc_s, sum_s = refs[-6:]
    first = info_ref[1]
    heads = q_ref.shape[-1] // HEAD
    scale = HEAD ** (-0.5)
    for head in range(heads):
        at = slice(head * HEAD, (head + 1) * HEAD)
        q_s[head * BLOCK : (head + 1) * BLOCK, :] = q_ref[0, :, at]
        d_s[head * BLOCK : (head + 1) * BLOCK, :] = d_ref[0, :, at]
    start = start_ref[0]
    key_iota = lax.broadcasted_iota(jnp.int32, (JOIN * BLOCK, BLOCK), 0)
    query_iota = lax.broadcasted_iota(jnp.int32, (JOIN * BLOCK, BLOCK), 1) + (WINDOW - 1) * BLOCK
    sum_s[...] = jnp.zeros_like(sum_s)
    acc_s[...] = jnp.zeros_like(acc_s)
    span = 2 * BLOCK
    spans = [slice(at, at + span) for at in range(0, heads * BLOCK, span)]

    def fold(array):
        return jnp.sum(array.reshape(JOIN * BLOCK // 8, 8, span), axis=0)

    for index in range(0, WINDOW, JOIN):
        at = slice(index * BLOCK, (index + JOIN) * BLOCK)

        @pl.when(index + JOIN > first)
        def _():
            key_pos = key_iota + index * BLOCK
            seen = (key_pos >= start) & (key_pos <= query_iota)
            bias = jnp.where(seen, 0.0, MASKED)
            bias = jnp.concatenate([bias, bias], axis=1)
            key = jnp.concatenate([k_refs[index + i][0] for i in range(JOIN)], axis=0)
            value = jnp.concatenate([v_refs[index + i][0] for i in range(JOIN)], axis=0)
            for cols in spans:
                scores = lax.dot_general(key, q_s[cols, :], NT, preferred_element_type=jnp.float32)
                dprobs = lax.dot_general(
                    value, d_s[cols, :], NT, preferred_element_type=jnp.float32
                )
                weights = jnp.exp2(scores * (scale * LOG2E) + bias)
                w_s[at, cols] = weights
                dp_s[at, cols] = dprobs
                sum_s[0:8, cols] += fold(weights)
                sum_s[8:16, cols] += fold(weights * dprobs)

    inverse = 1.0 / jnp.sum(sum_s[0:8, :], axis=0, keepdims=True)
    delta = jnp.sum(sum_s[8:16, :], axis=0, keepdims=True) * inverse

    for index in range(0, WINDOW, JOIN):
        at = slice(index * BLOCK, (index + JOIN) * BLOCK)
        joined = range(index, index + JOIN)

        @pl.when(index + JOIN <= first)
        def _():
            for i in joined:
                part_refs[i][0] = jnp.zeros(part_refs[i].shape[1:], jnp.bfloat16)

        @pl.when(index + JOIN > first)
        def _():
            key = [k_refs[i][0].astype(jnp.float32).T.astype(jnp.bfloat16) for i in joined]
            key = jnp.concatenate(key, axis=1)
            dk = jnp.zeros((JOIN * BLOCK, HEAD), jnp.float32)
            dv = jnp.zeros((JOIN * BLOCK, HEAD), jnp.float32)
            for cols in spans:
                probs = w_s[at, cols] * inverse[:, cols]
                dscores = (probs * (dp_s[at, cols] - delta[:, cols]) * scale).astype(jnp.bfloat16)
                dv += jnp.dot(
                    probs.astype(jnp.bfloat16), d_s[cols, :], preferred_element_type=jnp.float32
                )
                dk += jnp.dot(dscores, q_s[cols, :], preferred_element_type=jnp.float32)
                acc_s[:, cols] += jnp.dot(key, dscores, preferred_element_type=jnp.float32)
            for i in joined:
                rows = slice((i - index) * BLOCK, (i - index + 1) * BLOCK)
                part_refs[i][0, :, :HEAD] = dk[rows].astype(jnp.bfloat16)
                part_refs[i][0, :, HEAD:] = dv[rows].astype(jnp.bfloat16)

    for head in range(heads):
        at = slice(head * HEAD, (head + 1) * HEAD)
        dq_ref[0, :, at] = acc_s[:, head * BLOCK : (head + 1) * BLOCK].T.astype(jnp.bfloat16)


def attention(info, page, blocks, start, chunk, dq, parts, held_back=(), dq_width=4096):
    _, toks, page_width = page.shape
    rows = start.shape[0]
    width = dq_width // GROUPS
    first = chunk * SHARE if page_width == dq_width else 0
    queries = width // HEAD * toks
    pairs = SHARE * queries * WINDOW * BLOCK
    in_specs = [
        pl.BlockSpec((1, toks, width), lambda g, f: (0, 0, first + g)),
        pl.BlockSpec((1, toks, width), lambda g, f: (1, 0, first + g)),
    ]
    in_specs += [pl.BlockSpec((1, BLOCK, HEAD), lambda g, f: (f[0], 0, chunk * SHARE + g))] * WINDOW
    in_specs += [
        pl.BlockSpec((1, BLOCK, HEAD), lambda g, f: (f[0], 0, GROUPS + chunk * SHARE + g))
    ] * WINDOW
    in_specs += [pl.BlockSpec((1, 1, toks), lambda g, f: (f[0], 0, 0))]
    args = [page, page] + list(blocks) + list(blocks) + [start]
    aliases = {}
    for place, array in enumerate([dq] + list(parts)):
        if array is not None:
            aliases[1 + len(args)] = place
            in_specs.append(ANYWHERE)
            args.append(array)
    in_specs += [ANYWHERE] * len(held_back)
    args += held_back
    part_shape = jax.ShapeDtypeStruct((rows, BLOCK, SHARE * 2 * HEAD), jnp.bfloat16)
    spec = pltpu.PrefetchScalarGridSpec(
        num_scalar_prefetch=1,
        grid=(SHARE,),
        in_specs=in_specs,
        out_specs=[pl.BlockSpec((1, toks, width), lambda g, f: (f[0], 0, chunk * SHARE + g))]
        + [pl.BlockSpec((1, BLOCK, 2 * HEAD), lambda g, f: (f[0], 0, g))] * WINDOW,
        scratch_shapes=[
            pltpu.VMEM((queries, HEAD), jnp.bfloat16),
            pltpu.VMEM((queries, HEAD), jnp.bfloat16),
            pltpu.VMEM((WINDOW * BLOCK, queries), jnp.float32),
            pltpu.VMEM((WINDOW * BLOCK, queries), jnp.float32),
            pltpu.VMEM((HEAD, queries), jnp.float32),
            pltpu.VMEM((16, queries), jnp.float32),
        ],
    )
    return pl.pallas_call(
        attention_kernel,
        grid_spec=spec,
        out_shape=[jax.ShapeDtypeStruct((rows, toks, GROUPS * width), jnp.bfloat16)]
        + [part_shape] * WINDOW,
        input_output_aliases=aliases,
        compiler_params=pltpu.CompilerParams(vmem_limit_bytes=VMEM),
        cost_estimate=pl.CostEstimate(
            flops=10 * pairs * HEAD, bytes_accessed=4 * 1024 * 1024, transcendentals=pairs
        ),
    )(info, *args)


def arrange_kernel(plan_ref, place_ref, *refs):
    sources, out_ref = refs[:-1], refs[-1]
    rank_me, z_me, low_me, high_me = (place_ref[i] for i in range(4))
    for rel, source in enumerate(sources):
        for page in range(2):
            rank = rank_me ^ rel
            slot = jnp.int32(page)
            for step in range(ROUNDS):
                to_rank = rank ^ (1 << step)
                goes = plan_ref[(rank ^ rank_me) * ROUNDS + step] == slot
                slot = jnp.where(goes, plan_ref[(to_rank ^ rank_me) * ROUNDS + step], slot)
                rank = jnp.where(goes, to_rank, rank)
            column = pl.multiple_of(((rank ^ rank_me) * 2 + slot) * BLOCK, BLOCK)
            data = source[page * BLOCK : (page + 1) * BLOCK, :].astype(jnp.float32)
            data = data.T.astype(jnp.bfloat16)
            for low in range(2):
                for high in range(2):
                    for z in range(4):
                        at = ((low * 2 + high) * 4 + z) * 32
                        to = (z ^ z_me) * 4 + (low ^ low_me) + (high ^ high_me) * 2
                        to = pl.multiple_of(to * 32, 32)
                        out_ref[pl.ds(to, 32), pl.ds(column, BLOCK)] = data[at : at + 32, :]


def arrange(plan_all, place, sources):
    rows, cols = sources[0].shape
    return pl.pallas_call(
        arrange_kernel,
        grid_spec=pltpu.PrefetchScalarGridSpec(
            num_scalar_prefetch=2,
            grid=(1,),
            in_specs=[pl.BlockSpec((rows, cols), lambda i, a, b: (0, 0))] * len(sources),
            out_specs=pl.BlockSpec((cols, rows * len(sources)), lambda i, a, b: (0, 0)),
        ),
        out_shape=jax.ShapeDtypeStruct((cols, rows * len(sources)), jnp.bfloat16),
        compiler_params=pltpu.CompilerParams(vmem_limit_bytes=VMEM),
        cost_estimate=pl.CostEstimate(flops=0, bytes_accessed=4 * 1024 * 1024, transcendentals=0),
    )(plan_all, place, *sources)


def product_kernel(x_ref, *refs):
    grads, outs = refs[:TEAM], refs[TEAM:]
    for z, out in enumerate(outs):
        rows = slice(z * 4 * 32, (z + 1) * 4 * 32)
        total = None
        for rel, grad in enumerate(grads):
            span = 2 * BLOCK
            block = jnp.concatenate([grad[0], grad[1]], axis=0)
            term = jnp.dot(
                x_ref[rows, rel * span : (rel + 1) * span],
                block,
                preferred_element_type=jnp.float32,
            )
            total = term if total is None else total + term
        out[...] = total.astype(out.dtype)


def product(x, grads):
    cols = grads[0].shape[-1]
    shape = (x.shape[0] // 4, cols)
    return pl.pallas_call(
        product_kernel,
        out_shape=[jax.ShapeDtypeStruct(shape, jnp.float32)]
        + [jax.ShapeDtypeStruct(shape, jnp.bfloat16)] * 3,
        compiler_params=pltpu.CompilerParams(vmem_limit_bytes=VMEM),
        cost_estimate=pl.CostEstimate(
            flops=2 * x.shape[0] * x.shape[1] * cols,
            bytes_accessed=5 * 1024 * 1024,
            transcendentals=0,
        ),
    )(x, *grads)


def per_device(tokens, queries, out_grad, kv_weight, doc_lengths, swap_plan):
    seqs, toks, width = tokens.shape
    pair = kv_weight.shape[1]
    cols = pair // 2
    group_width = queries.shape[2] // GROUPS
    dp = lax.axis_index("dp")
    ctx = lax.axis_index("ctx")
    rank = lax.rem(dp, TEAM)
    z = lax.rem(ctx, 4)
    y_high = ctx // 4
    y_low = dp // TEAM
    plan = swap_plan[0, 0]
    plans = jnp.stack([plan] + [move(plan, flip_dp(2 * k)) for k in range(1, TEAM // 2)])
    plan_all = jnp.stack([plans, move(plans, flip_dp(1))], axis=1).reshape(-1)

    ends = jnp.cumsum(doc_lengths, axis=1)
    pos = ctx * toks + jnp.arange(toks, dtype=jnp.int32)
    begun = jnp.max(
        jnp.where(ends[:, None, :] <= pos[None, :, None], ends[:, None, :], 0), axis=2
    )
    start = begun - (ctx - (WINDOW - 1)) * toks
    first = jnp.clip(start[:, 0] // BLOCK, 0, WINDOW - 1)
    start = start[:, None, :]
    row_came = plan[ROUNDS - 1]
    row_kept = 1 - row_came
    info_came = jnp.stack([row_came, jnp.where(row_came == 0, first[0], first[1])])
    info_kept = jnp.stack([row_kept, jnp.where(row_kept == 0, first[0], first[1])])

    def cross(step, value):
        return move(value, flip_dp(1 << step))

    halves = [queries, out_grad]
    flat = tokens.reshape(seqs * toks, width)
    kv = jnp.dot(flat, kv_weight, preferred_element_type=jnp.float32).astype(jnp.bfloat16)
    kv = kv.reshape(seqs, toks, pair)
    kv_came = cross(0, pages_of(plan, [kv], [plan_all])[0])
    send = second_pages_of(plan, [kv_came], [kv])
    loaded = [cross(0, one) for one in pages_of(plan, halves, [send])]
    kv_second = cross(1, send)
    send, kv_kept = third_pages_of(plan, kv_second, [kv_came], [kv], 0, 1, True)
    kv_third = cross(2, send)
    send = second_pages_of(plan, loaded, halves)
    send = hold(send, kv_third)
    came = cross(1, send)
    own = rows_of(plan, kv_third, kv_kept, [send])
    near = [move(own, shift_z(by)) for by in (1, 2, 3)]
    above = move(own, lift)
    far = [
        move(above, shift_z(1, {(1, 0), (1, 1), (1, 2), (1, 3)}, True)),
        move(above, shift_z(2, {(1, 2), (1, 3)}, True)),
        move(above, shift_z(3, {(1, 1), (1, 2), (1, 3)}, True)),
    ]
    blocks = [
        far[0],
        above,
        near[2] + far[2],
        near[1] + far[1],
        jnp.where(z == 0, far[0], near[0]),
        own,
    ]
    send_a, kept = third_pages_of(
        plan, came, loaded, halves, 0, CHUNKS, True, held_back=near + far
    )
    came_a = cross(2, send_a)
    none = [None] * WINDOW

    def collect(parts):
        return parts[-1:] + [
            move(parts[WINDOW - 1 - by], shift_ctx(-by)) for by in range(1, WINDOW)
        ]

    there = [None] * (TEAM // 2)
    there[0], column = columns_of(rank[None], flat, [0, 2], [send_a])
    there[2] = move(column, flip_dp(4))
    dq, *parts_a = attention(info_kept, kept, blocks, start, 0, None, none)
    dq, *parts_b = attention(info_kept, kept, blocks, start, 1, dq, none)
    send_b = third_pages_of(
        plan, came, loaded, halves, 1, CHUNKS, False, held_back=[came_a, parts_b[0], there[2]]
    )[0]
    came_b = cross(2, send_b)
    dq, *parts_a = attention(info_came, came_a, blocks, start, 0, dq, parts_a)
    parts_a = collect(parts_a)
    columns = list(columns_of(rank[None], flat, [1, 3], [came_b]))
    for k, column in zip((1, 3), columns):
        there[k] = move(column, flip_dp(2 * k))
    dq, *parts_b = attention(
        info_came, came_b, blocks, start, 1, dq, parts_b, parts_a[1:4] + columns[:1]
    )
    grad = sum_of([parts_a, collect(parts_b)], [there[1], there[3]])

    sources = []
    for k in range(TEAM // 2):
        sources += [there[k][0], move(there[k][1], flip_dp(1))]
    place = jnp.stack([rank, z, y_low, y_high])
    arranged = arrange(plan_all, place, sources)
    grads = []
    for k in range(TEAM // 2):
        chip = move(grad, flip_dp(2 * k)) if k else grad
        grads += [chip, move(chip, flip_dp(1))]
    mine, *others = product(arranged, grads)
    for k, other in enumerate(others):
        mine = mine + move(other, flip_ctx(k + 1)).astype(jnp.float32)
    final = mine[:32]
    for k in range(1, 4):
        final = final + move(mine[32 * k : 32 * (k + 1)], flip_y(k % 2, k // 2))
    return dq, final


def solution(mesh):
    in_specs = (
        P("dp", "ctx", None),
        P("dp", "ctx", None),
        P("dp", "ctx", None),
        P(),
        P("dp", None),
        P("dp", "ctx", None),
    )
    out_specs = (P("dp", "ctx", None), P(("dp", "ctx"), None))
    return jax.shard_map(
        per_device, mesh=mesh, in_specs=in_specs, out_specs=out_specs, check_vma=False
    )
```

```python
import functools

import jax
import jax.numpy as jnp
from jax import lax
from jax.experimental import pallas as pl
from jax.experimental.pallas import tpu as pltpu
from jax.sharding import PartitionSpec as P

HEAD = 128
ROUNDS = 3
AXES = ("dp", "ctx")
N_DP = 16
N_CTX = 8
TEAM = 8
WINDOW = 6
BLOCK = 128
GROUPS = 4
CHUNKS = 2
SHARE = GROUPS // CHUNKS
VMEM = 48 * 1024 * 1024
MASKED = -1e30
JOIN = 6
LOG2E = 1.4426950408889634
NT = (((1,), (1,)), ((), ()))


def move(value, target):
    route = []
    for dp in range(N_DP):
        for ctx in range(N_CTX):
            to_dp, to_ctx = target(dp, ctx)
            if 0 <= to_ctx < N_CTX:
                route.append((dp * N_CTX + ctx, to_dp * N_CTX + to_ctx))
    return lax.ppermute(value, AXES, route)


def flip_dp(bits):
    return lambda dp, ctx: (dp ^ bits, ctx)


def flip_ctx(bits):
    return lambda dp, ctx: (dp, ctx ^ bits)


def shift_ctx(by):
    return lambda dp, ctx: (dp, ctx + by)


def shift_z(by, only=None, around=False):
    def target(dp, ctx):
        high, z = ctx // 4, ctx % 4
        if only is not None and (high, z) not in only:
            return dp, -1
        if not around and z + by > 3:
            return dp, -1
        return dp, high * 4 + (z + by) % 4

    return target


def lift(dp, ctx):
    return dp, ctx + 4


def flip_y(low, high):
    return lambda dp, ctx: (dp ^ (low * 8), ctx ^ (high * 4))


ANYWHERE = pl.BlockSpec(memory_space=pl.ANY)


def light(read):
    return dict(
        compiler_params=pltpu.CompilerParams(vmem_limit_bytes=VMEM),
        cost_estimate=pl.CostEstimate(flops=0, bytes_accessed=read, transcendentals=0),
    )


def copy_all(sems, pairs):
    copies = [
        pltpu.make_async_copy(source, target, sems.at[i])
        for i, (source, target) in enumerate(pairs)
    ]
    for copy in copies:
        copy.start()
    for copy in copies:
        copy.wait()


def copier(kernel, shapes, count, plan, *arrays):
    return pl.pallas_call(
        kernel,
        in_specs=[pl.BlockSpec(memory_space=pltpu.SMEM)] + [ANYWHERE] * len(arrays),
        out_specs=[pl.BlockSpec(memory_space=pltpu.VMEM)] * len(shapes),
        out_shape=[jax.ShapeDtypeStruct(shape, jnp.bfloat16) for shape in shapes],
        scratch_shapes=[pltpu.SemaphoreType.DMA((count,))],
        compiler_params=pltpu.CompilerParams(vmem_limit_bytes=VMEM),
        cost_estimate=pl.CostEstimate(flops=0, bytes_accessed=4 * 1024 * 1024, transcendentals=0),
    )(plan, *arrays)


def pages_of(plan, arrays, held_back=()):
    count = len(arrays)

    def kernel(plan_ref, *refs):
        outs, sems = refs[-1 - count : -1], refs[-1]
        copy_all(sems, [(ref.at[plan_ref[0]], out) for ref, out in zip(refs, outs)])

    return copier(kernel, [array.shape[1:] for array in arrays], count, plan, *arrays, *held_back)


def second_pages_of(plan, came, loaded, held_back=()):
    count = len(came)

    def kernel(plan_ref, *refs):
        out, sems = refs[-2], refs[-1]
        outs = [out.at[i] for i in range(count)]
        same = plan_ref[1] == plan_ref[0]

        @pl.when(same)
        def _():
            copy_all(sems, list(zip(refs[:count], outs)))

        @pl.when(jnp.logical_not(same))
        def _():
            others = [ref.at[1 - plan_ref[0]] for ref in refs[count : 2 * count]]
            copy_all(sems, list(zip(others, outs)))

    shape = (count,) + came[0].shape
    return copier(kernel, [shape], count, plan, *came, *loaded, *held_back)[0]


def third_pages_of(plan, came, came_before, loaded, part, parts, stays, held_back=()):
    count, toks, width = came.shape
    at = pl.ds(part * (width // parts), width // parts)
    whole = pl.ds(0, width)

    def kernel(plan_ref, came_ref, *refs):
        before, pages = refs[:count], refs[count : 2 * count]
        outs, sems = refs[-3 if stays else -2 : -1], refs[-1]
        first = plan_ref[1] == plan_ref[0]
        same = plan_ref[2] == plan_ref[1]

        def new(i, cols):
            return came_ref.at[i, :, cols]

        def old_from(came_first):
            def old(i, cols):
                if came_first:
                    return pages[i].at[1 - plan_ref[0], :, cols]
                return before[i].at[:, cols]

            return old

        for again in (True, False):
            for came_first in (True, False):

                @pl.when((same == again) & (first == came_first))
                def _():
                    old = old_from(came_first)
                    sources = (new, old) if again else (old, new)
                    pairs = [(sources[0](i, at), outs[0].at[i]) for i in range(count)]
                    if stays:
                        pairs += [(sources[1](i, whole), outs[1].at[i]) for i in range(count)]
                    copy_all(sems, pairs)

    shapes = [(count, toks, width // parts)] + [came.shape] * stays
    return copier(
        kernel, shapes, 2 * count, plan, came, *came_before, *loaded, *held_back
    )


def rows_of(plan, came, kept, held_back=()):
    def kernel(plan_ref, came_ref, kept_ref, *refs):
        out, sems = refs[-2:]
        slot = plan_ref[ROUNDS - 1]
        copy_all(sems, [(came_ref.at[0], out.at[slot]), (kept_ref.at[0], out.at[1 - slot])])

    return copier(kernel, [(2,) + came.shape[1:]], 2, plan, came, kept, *held_back)[0]


def sum_kernel(*refs):
    out_ref = refs[-1]
    half = out_ref.shape[-1] // 2
    for chunk in range(CHUNKS):
        parts = refs[chunk * WINDOW : (chunk + 1) * WINDOW]
        for group in range(SHARE):
            for kind in range(2):
                at = (group * 2 + kind) * HEAD
                to = kind * half + (chunk * SHARE + group) * HEAD
                total = parts[0][:, :, at : at + HEAD].astype(jnp.float32)
                for part in parts[1:]:
                    total = total + part[:, :, at : at + HEAD].astype(jnp.float32)
                out_ref[:, :, to : to + HEAD] = total.astype(out_ref.dtype)


def sum_of(chunks, held_back=()):
    vmem = pl.BlockSpec(memory_space=pltpu.VMEM)
    rows, toks, cols = chunks[0][0].shape
    return pl.pallas_call(
        sum_kernel,
        in_specs=[vmem] * (WINDOW * CHUNKS) + [ANYWHERE] * len(held_back),
        out_specs=vmem,
        out_shape=jax.ShapeDtypeStruct((rows, toks, cols * CHUNKS), jnp.bfloat16),
        **light(4 * 1024 * 1024),
    )(*[part for parts in chunks for part in parts], *held_back)


def columns_kernel(count, place_ref, *refs):
    sources, outs = refs[: 4 * count], refs[-count:]
    part = sources[0].shape[1]
    for k, out in enumerate(outs):
        for side in range(2):
            for low in range(2):
                out[side, :, low * part : (low + 1) * part] = sources[(k * 2 + side) * 2 + low][...]


def columns_of(place, flat, chips, held_back=()):
    rows, width = flat.shape
    part = width // (2 * TEAM)
    in_specs = []
    for k in chips:
        for side in range(2):
            for low in range(2):
                in_specs.append(
                    pl.BlockSpec(
                        (rows, part),
                        lambda i, p, bits=2 * k + side, low=low: (0, low * TEAM + (p[0] ^ bits)),
                    )
                )
    shape = jax.ShapeDtypeStruct((2, rows, 2 * part), flat.dtype)
    out = pl.BlockSpec((2, rows, 2 * part), lambda i, p: (0, 0, 0))
    return pl.pallas_call(
        functools.partial(columns_kernel, len(chips)),
        grid_spec=pltpu.PrefetchScalarGridSpec(
            num_scalar_prefetch=1,
            grid=(1,),
            in_specs=in_specs + [ANYWHERE] * len(held_back),
            out_specs=[out] * len(chips),
        ),
        out_shape=[shape] * len(chips),
        **light(1024 * 1024),
    )(place, *([flat] * len(in_specs)), *held_back)


def hold_kernel(*refs):
    pass


def hold(array, *held_back):
    return pl.pallas_call(
        hold_kernel,
        in_specs=[ANYWHERE] * (1 + len(held_back)),
        out_specs=ANYWHERE,
        out_shape=jax.ShapeDtypeStruct(array.shape, array.dtype),
        input_output_aliases={0: 0},
        **light(1024),
    )(array, *held_back)


def attention_kernel(info_ref, *refs):
    q_ref, d_ref = refs[:2]
    k_refs = refs[2 : 2 + WINDOW]
    v_refs = refs[2 + WINDOW : 2 + 2 * WINDOW]
    start_ref = refs[2 + 2 * WINDOW]
    outs = len(refs) - 7 - WINDOW
    dq_ref = refs[outs]
    part_refs = refs[outs + 1 : outs + 1 + WINDOW]
    q_s, d_s, w_s, dp_s, acc_s, sum_s = refs[-6:]
    first = info_ref[1]
    heads = q_ref.shape[-1] // HEAD
    scale = HEAD ** (-0.5)
    for head in range(heads):
        at = slice(head * HEAD, (head + 1) * HEAD)
        q_s[head * BLOCK : (head + 1) * BLOCK, :] = q_ref[0, :, at]
        d_s[head * BLOCK : (head + 1) * BLOCK, :] = d_ref[0, :, at]
    start = start_ref[0]
    key_iota = lax.broadcasted_iota(jnp.int32, (JOIN * BLOCK, BLOCK), 0)
    query_iota = lax.broadcasted_iota(jnp.int32, (JOIN * BLOCK, BLOCK), 1) + (WINDOW - 1) * BLOCK
    sum_s[...] = jnp.zeros_like(sum_s)
    acc_s[...] = jnp.zeros_like(acc_s)
    span = 2 * BLOCK
    spans = [slice(at, at + span) for at in range(0, heads * BLOCK, span)]

    def fold(array):
        return jnp.sum(array.reshape(JOIN * BLOCK // 8, 8, span), axis=0)

    for index in range(0, WINDOW, JOIN):
        at = slice(index * BLOCK, (index + JOIN) * BLOCK)

        @pl.when(index + JOIN > first)
        def _():
            key_pos = key_iota + index * BLOCK
            seen = (key_pos >= start) & (key_pos <= query_iota)
            bias = jnp.where(seen, 0.0, MASKED)
            bias = jnp.concatenate([bias, bias], axis=1)
            key = jnp.concatenate([k_refs[index + i][0] for i in range(JOIN)], axis=0)
            value = jnp.concatenate([v_refs[index + i][0] for i in range(JOIN)], axis=0)
            for cols in spans:
                scores = lax.dot_general(key, q_s[cols, :], NT, preferred_element_type=jnp.float32)
                dprobs = lax.dot_general(
                    value, d_s[cols, :], NT, preferred_element_type=jnp.float32
                )
                weights = jnp.exp2(scores * (scale * LOG2E) + bias)
                w_s[at, cols] = weights
                dp_s[at, cols] = dprobs
                sum_s[0:8, cols] += fold(weights)
                sum_s[8:16, cols] += fold(weights * dprobs)

    inverse = 1.0 / jnp.sum(sum_s[0:8, :], axis=0, keepdims=True)
    delta = jnp.sum(sum_s[8:16, :], axis=0, keepdims=True) * inverse

    for index in range(0, WINDOW, JOIN):
        at = slice(index * BLOCK, (index + JOIN) * BLOCK)
        joined = range(index, index + JOIN)

        @pl.when(index + JOIN <= first)
        def _():
            for i in joined:
                part_refs[i][0] = jnp.zeros(part_refs[i].shape[1:], jnp.bfloat16)

        @pl.when(index + JOIN > first)
        def _():
            key = [k_refs[i][0].astype(jnp.float32).T.astype(jnp.bfloat16) for i in joined]
            key = jnp.concatenate(key, axis=1)
            dk = jnp.zeros((JOIN * BLOCK, HEAD), jnp.float32)
            dv = jnp.zeros((JOIN * BLOCK, HEAD), jnp.float32)
            for cols in spans:
                probs = w_s[at, cols] * inverse[:, cols]
                dscores = (probs * (dp_s[at, cols] - delta[:, cols]) * scale).astype(jnp.bfloat16)
                dv += jnp.dot(
                    probs.astype(jnp.bfloat16), d_s[cols, :], preferred_element_type=jnp.float32
                )
                dk += jnp.dot(dscores, q_s[cols, :], preferred_element_type=jnp.float32)
                acc_s[:, cols] += jnp.dot(key, dscores, preferred_element_type=jnp.float32)
            for i in joined:
                rows = slice((i - index) * BLOCK, (i - index + 1) * BLOCK)
                part_refs[i][0, :, :HEAD] = dk[rows].astype(jnp.bfloat16)
                part_refs[i][0, :, HEAD:] = dv[rows].astype(jnp.bfloat16)

    for head in range(heads):
        at = slice(head * HEAD, (head + 1) * HEAD)
        dq_ref[0, :, at] = acc_s[:, head * BLOCK : (head + 1) * BLOCK].T.astype(jnp.bfloat16)


def attention(info, page, blocks, start, chunk, dq, parts, held_back=(), dq_width=4096):
    _, toks, page_width = page.shape
    rows = start.shape[0]
    width = dq_width // GROUPS
    first = chunk * SHARE if page_width == dq_width else 0
    queries = width // HEAD * toks
    pairs = SHARE * queries * WINDOW * BLOCK
    in_specs = [
        pl.BlockSpec((1, toks, width), lambda g, f: (0, 0, first + g)),
        pl.BlockSpec((1, toks, width), lambda g, f: (1, 0, first + g)),
    ]
    in_specs += [pl.BlockSpec((1, BLOCK, HEAD), lambda g, f: (f[0], 0, chunk * SHARE + g))] * WINDOW
    in_specs += [
        pl.BlockSpec((1, BLOCK, HEAD), lambda g, f: (f[0], 0, GROUPS + chunk * SHARE + g))
    ] * WINDOW
    in_specs += [pl.BlockSpec((1, 1, toks), lambda g, f: (f[0], 0, 0))]
    args = [page, page] + list(blocks) + list(blocks) + [start]
    aliases = {}
    for place, array in enumerate([dq] + list(parts)):
        if array is not None:
            aliases[1 + len(args)] = place
            in_specs.append(ANYWHERE)
            args.append(array)
    in_specs += [ANYWHERE] * len(held_back)
    args += held_back
    part_shape = jax.ShapeDtypeStruct((rows, BLOCK, SHARE * 2 * HEAD), jnp.bfloat16)
    spec = pltpu.PrefetchScalarGridSpec(
        num_scalar_prefetch=1,
        grid=(SHARE,),
        in_specs=in_specs,
        out_specs=[pl.BlockSpec((1, toks, width), lambda g, f: (f[0], 0, chunk * SHARE + g))]
        + [pl.BlockSpec((1, BLOCK, 2 * HEAD), lambda g, f: (f[0], 0, g))] * WINDOW,
        scratch_shapes=[
            pltpu.VMEM((queries, HEAD), jnp.bfloat16),
            pltpu.VMEM((queries, HEAD), jnp.bfloat16),
            pltpu.VMEM((WINDOW * BLOCK, queries), jnp.float32),
            pltpu.VMEM((WINDOW * BLOCK, queries), jnp.float32),
            pltpu.VMEM((HEAD, queries), jnp.float32),
            pltpu.VMEM((16, queries), jnp.float32),
        ],
    )
    return pl.pallas_call(
        attention_kernel,
        grid_spec=spec,
        out_shape=[jax.ShapeDtypeStruct((rows, toks, GROUPS * width), jnp.bfloat16)]
        + [part_shape] * WINDOW,
        input_output_aliases=aliases,
        compiler_params=pltpu.CompilerParams(vmem_limit_bytes=VMEM),
        cost_estimate=pl.CostEstimate(
            flops=10 * pairs * HEAD, bytes_accessed=4 * 1024 * 1024, transcendentals=pairs
        ),
    )(info, *args)


def arrange_kernel(plan_ref, place_ref, *refs):
    sources, out_ref = refs[:-1], refs[-1]
    rank_me, z_me, low_me, high_me = (place_ref[i] for i in range(4))
    for rel, source in enumerate(sources):
        for page in range(2):
            rank = rank_me ^ rel
            slot = jnp.int32(page)
            for step in range(ROUNDS):
                to_rank = rank ^ (1 << step)
                goes = plan_ref[(rank ^ rank_me) * ROUNDS + step] == slot
                slot = jnp.where(goes, plan_ref[(to_rank ^ rank_me) * ROUNDS + step], slot)
                rank = jnp.where(goes, to_rank, rank)
            column = pl.multiple_of(((rank ^ rank_me) * 2 + slot) * BLOCK, BLOCK)
            data = source[page * BLOCK : (page + 1) * BLOCK, :].astype(jnp.float32)
            data = data.T.astype(jnp.bfloat16)
            for low in range(2):
                for high in range(2):
                    for z in range(4):
                        at = ((low * 2 + high) * 4 + z) * 32
                        to = (z ^ z_me) * 4 + (low ^ low_me) + (high ^ high_me) * 2
                        to = pl.multiple_of(to * 32, 32)
                        out_ref[pl.ds(to, 32), pl.ds(column, BLOCK)] = data[at : at + 32, :]


def arrange(plan_all, place, sources):
    rows, cols = sources[0].shape
    return pl.pallas_call(
        arrange_kernel,
        grid_spec=pltpu.PrefetchScalarGridSpec(
            num_scalar_prefetch=2,
            grid=(1,),
            in_specs=[pl.BlockSpec((rows, cols), lambda i, a, b: (0, 0))] * len(sources),
            out_specs=pl.BlockSpec((cols, rows * len(sources)), lambda i, a, b: (0, 0)),
        ),
        out_shape=jax.ShapeDtypeStruct((cols, rows * len(sources)), jnp.bfloat16),
        compiler_params=pltpu.CompilerParams(vmem_limit_bytes=VMEM),
        cost_estimate=pl.CostEstimate(flops=0, bytes_accessed=4 * 1024 * 1024, transcendentals=0),
    )(plan_all, place, *sources)


def product_kernel(x_ref, *refs):
    grads, outs = refs[:TEAM], refs[TEAM:]
    for z, out in enumerate(outs):
        rows = slice(z * 4 * 32, (z + 1) * 4 * 32)
        total = None
        for rel, grad in enumerate(grads):
            span = 2 * BLOCK
            block = jnp.concatenate([grad[0], grad[1]], axis=0)
            term = jnp.dot(
                x_ref[rows, rel * span : (rel + 1) * span],
                block,
                preferred_element_type=jnp.float32,
            )
            total = term if total is None else total + term
        out[...] = total.astype(out.dtype)


def product(x, grads):
    cols = grads[0].shape[-1]
    shape = (x.shape[0] // 4, cols)
    return pl.pallas_call(
        product_kernel,
        out_shape=[jax.ShapeDtypeStruct(shape, jnp.float32)]
        + [jax.ShapeDtypeStruct(shape, jnp.bfloat16)] * 3,
        compiler_params=pltpu.CompilerParams(vmem_limit_bytes=VMEM),
        cost_estimate=pl.CostEstimate(
            flops=2 * x.shape[0] * x.shape[1] * cols,
            bytes_accessed=5 * 1024 * 1024,
            transcendentals=0,
        ),
    )(x, *grads)


def per_device(tokens, queries, out_grad, kv_weight, doc_lengths, swap_plan):
    seqs, toks, width = tokens.shape
    pair = kv_weight.shape[1]
    cols = pair // 2
    group_width = queries.shape[2] // GROUPS
    dp = lax.axis_index("dp")
    ctx = lax.axis_index("ctx")
    rank = lax.rem(dp, TEAM)
    z = lax.rem(ctx, 4)
    y_high = ctx // 4
    y_low = dp // TEAM
    plan = swap_plan[0, 0]
    plans = jnp.stack([plan] + [move(plan, flip_dp(2 * k)) for k in range(1, TEAM // 2)])
    plan_all = jnp.stack([plans, move(plans, flip_dp(1))], axis=1).reshape(-1)

    ends = jnp.cumsum(doc_lengths, axis=1)
    pos = ctx * toks + jnp.arange(toks, dtype=jnp.int32)
    begun = jnp.max(
        jnp.where(ends[:, None, :] <= pos[None, :, None], ends[:, None, :], 0), axis=2
    )
    start = begun - (ctx - (WINDOW - 1)) * toks
    first = jnp.clip(start[:, 0] // BLOCK, 0, WINDOW - 1)
    start = start[:, None, :]
    row_came = plan[ROUNDS - 1]
    row_kept = 1 - row_came
    info_came = jnp.stack([row_came, jnp.where(row_came == 0, first[0], first[1])])
    info_kept = jnp.stack([row_kept, jnp.where(row_kept == 0, first[0], first[1])])

    def cross(step, value):
        return move(value, flip_dp(1 << step))

    halves = [queries, out_grad]
    flat = tokens.reshape(seqs * toks, width)
    kv = jnp.dot(flat, kv_weight, preferred_element_type=jnp.float32).astype(jnp.bfloat16)
    kv = kv.reshape(seqs, toks, pair)
    kv_came = cross(0, pages_of(plan, [kv], [plan_all])[0])
    send = second_pages_of(plan, [kv_came], [kv])
    loaded = [cross(0, one) for one in pages_of(plan, halves, [send])]
    kv_second = cross(1, send)
    send, kv_kept = third_pages_of(plan, kv_second, [kv_came], [kv], 0, 1, True)
    kv_third = cross(2, send)
    send = second_pages_of(plan, loaded, halves)
    send = hold(send, kv_third)
    came = cross(1, send)
    own = rows_of(plan, kv_third, kv_kept, [send])
    near = [move(own, shift_z(by)) for by in (1, 2, 3)]
    above = move(own, lift)
    far = [
        move(above, shift_z(1, {(1, 0), (1, 1), (1, 2), (1, 3)}, True)),
        move(above, shift_z(2, {(1, 2), (1, 3)}, True)),
        move(above, shift_z(3, {(1, 1), (1, 2), (1, 3)}, True)),
    ]
    blocks = [
        far[0],
        above,
        near[2] + far[2],
        near[1] + far[1],
        jnp.where(z == 0, far[0], near[0]),
        own,
    ]
    send_a, kept = third_pages_of(
        plan, came, loaded, halves, 0, CHUNKS, True, held_back=near + far
    )
    came_a = cross(2, send_a)
    none = [None] * WINDOW

    def collect(parts):
        return parts[-1:] + [
            move(parts[WINDOW - 1 - by], shift_ctx(-by)) for by in range(1, WINDOW)
        ]

    there = [None] * (TEAM // 2)
    there[0], column = columns_of(rank[None], flat, [0, 2], [send_a])
    there[2] = move(column, flip_dp(4))
    dq, *parts_a = attention(info_kept, kept, blocks, start, 0, None, none)
    dq, *parts_b = attention(info_kept, kept, blocks, start, 1, dq, none)
    send_b = third_pages_of(
        plan, came, loaded, halves, 1, CHUNKS, False, held_back=[came_a, parts_b[0], there[2]]
    )[0]
    came_b = cross(2, send_b)
    dq, *parts_a = attention(info_came, came_a, blocks, start, 0, dq, parts_a)
    parts_a = collect(parts_a)
    columns = list(columns_of(rank[None], flat, [1, 3], [came_b]))
    for k, column in zip((1, 3), columns):
        there[k] = move(column, flip_dp(2 * k))
    dq, *parts_b = attention(
        info_came, came_b, blocks, start, 1, dq, parts_b, parts_a[1:4] + columns[:1]
    )
    sources = []
    for k in range(TEAM // 2):
        sources += [there[k][0], move(there[k][1], flip_dp(1))]
    place = jnp.stack([rank, z, y_low, y_high])
    arranged = arrange(plan_all, place, sources)
    grad = sum_of([parts_a, collect(parts_b)], [arranged])

    grads = []
    for k in range(TEAM // 2):
        chip = move(grad, flip_dp(2 * k)) if k else grad
        grads += [chip, move(chip, flip_dp(1))]
    mine, *others = product(arranged, grads)
    for k, other in enumerate(others):
        mine = mine + move(other, flip_ctx(k + 1)).astype(jnp.float32)
    final = mine[:32]
    for k in range(1, 4):
        final = final + move(mine[32 * k : 32 * (k + 1)], flip_y(k % 2, k // 2))
    return dq, final


def solution(mesh):
    in_specs = (
        P("dp", "ctx", None),
        P("dp", "ctx", None),
        P("dp", "ctx", None),
        P(),
        P("dp", None),
        P("dp", "ctx", None),
    )
    out_specs = (P("dp", "ctx", None), P(("dp", "ctx"), None))
    return jax.shard_map(
        per_device, mesh=mesh, in_specs=in_specs, out_specs=out_specs, check_vma=False
    )
```

```python
import functools

import jax
import jax.numpy as jnp
from jax import lax
from jax.experimental import pallas as pl
from jax.experimental.pallas import tpu as pltpu
from jax.sharding import PartitionSpec as P

HEAD = 128
ROUNDS = 3
AXES = ("dp", "ctx")
N_DP = 16
N_CTX = 8
TEAM = 8
WINDOW = 6
BLOCK = 128
GROUPS = 4
CHUNKS = 2
SHARE = GROUPS // CHUNKS
VMEM = 48 * 1024 * 1024
MASKED = -1e30
JOIN = 6
LOG2E = 1.4426950408889634
NT = (((1,), (1,)), ((), ()))


def move(value, target):
    route = []
    for dp in range(N_DP):
        for ctx in range(N_CTX):
            to_dp, to_ctx = target(dp, ctx)
            if 0 <= to_ctx < N_CTX:
                route.append((dp * N_CTX + ctx, to_dp * N_CTX + to_ctx))
    return lax.ppermute(value, AXES, route)


def flip_dp(bits):
    return lambda dp, ctx: (dp ^ bits, ctx)


def flip_ctx(bits):
    return lambda dp, ctx: (dp, ctx ^ bits)


def shift_ctx(by):
    return lambda dp, ctx: (dp, ctx + by)


def shift_z(by, only=None, around=False):
    def target(dp, ctx):
        high, z = ctx // 4, ctx % 4
        if only is not None and (high, z) not in only:
            return dp, -1
        if not around and z + by > 3:
            return dp, -1
        return dp, high * 4 + (z + by) % 4

    return target


def lift(dp, ctx):
    return dp, ctx + 4


def flip_y(low, high):
    return lambda dp, ctx: (dp ^ (low * 8), ctx ^ (high * 4))


ANYWHERE = pl.BlockSpec(memory_space=pl.ANY)


def light(read):
    return dict(
        compiler_params=pltpu.CompilerParams(vmem_limit_bytes=VMEM),
        cost_estimate=pl.CostEstimate(flops=0, bytes_accessed=read, transcendentals=0),
    )


def copy_all(sems, pairs):
    copies = [
        pltpu.make_async_copy(source, target, sems.at[i])
        for i, (source, target) in enumerate(pairs)
    ]
    for copy in copies:
        copy.start()
    for copy in copies:
        copy.wait()


def copier(kernel, shapes, count, plan, *arrays):
    return pl.pallas_call(
        kernel,
        in_specs=[pl.BlockSpec(memory_space=pltpu.SMEM)] + [ANYWHERE] * len(arrays),
        out_specs=[pl.BlockSpec(memory_space=pltpu.VMEM)] * len(shapes),
        out_shape=[jax.ShapeDtypeStruct(shape, jnp.bfloat16) for shape in shapes],
        scratch_shapes=[pltpu.SemaphoreType.DMA((count,))],
        compiler_params=pltpu.CompilerParams(vmem_limit_bytes=VMEM),
        cost_estimate=pl.CostEstimate(flops=0, bytes_accessed=4 * 1024 * 1024, transcendentals=0),
    )(plan, *arrays)


def pages_of(plan, arrays, held_back=()):
    count = len(arrays)

    def kernel(plan_ref, *refs):
        outs, sems = refs[-1 - count : -1], refs[-1]
        copy_all(sems, [(ref.at[plan_ref[0]], out) for ref, out in zip(refs, outs)])

    return copier(kernel, [array.shape[1:] for array in arrays], count, plan, *arrays, *held_back)


def second_pages_of(plan, came, loaded, held_back=()):
    count = len(came)

    def kernel(plan_ref, *refs):
        out, sems = refs[-2], refs[-1]
        outs = [out.at[i] for i in range(count)]
        same = plan_ref[1] == plan_ref[0]

        @pl.when(same)
        def _():
            copy_all(sems, list(zip(refs[:count], outs)))

        @pl.when(jnp.logical_not(same))
        def _():
            others = [ref.at[1 - plan_ref[0]] for ref in refs[count : 2 * count]]
            copy_all(sems, list(zip(others, outs)))

    shape = (count,) + came[0].shape
    return copier(kernel, [shape], count, plan, *came, *loaded, *held_back)[0]


def third_pages_of(plan, came, came_before, loaded, part, parts, stays, held_back=()):
    count, toks, width = came.shape
    at = pl.ds(part * (width // parts), width // parts)
    whole = pl.ds(0, width)

    def kernel(plan_ref, came_ref, *refs):
        before, pages = refs[:count], refs[count : 2 * count]
        outs, sems = refs[-3 if stays else -2 : -1], refs[-1]
        first = plan_ref[1] == plan_ref[0]
        same = plan_ref[2] == plan_ref[1]

        def new(i, cols):
            return came_ref.at[i, :, cols]

        def old_from(came_first):
            def old(i, cols):
                if came_first:
                    return pages[i].at[1 - plan_ref[0], :, cols]
                return before[i].at[:, cols]

            return old

        for again in (True, False):
            for came_first in (True, False):

                @pl.when((same == again) & (first == came_first))
                def _():
                    old = old_from(came_first)
                    sources = (new, old) if again else (old, new)
                    pairs = [(sources[0](i, at), outs[0].at[i]) for i in range(count)]
                    if stays:
                        pairs += [(sources[1](i, whole), outs[1].at[i]) for i in range(count)]
                    copy_all(sems, pairs)

    shapes = [(count, toks, width // parts)] + [came.shape] * stays
    return copier(
        kernel, shapes, 2 * count, plan, came, *came_before, *loaded, *held_back
    )


def rows_of(plan, came, kept, held_back=()):
    def kernel(plan_ref, came_ref, kept_ref, *refs):
        out, sems = refs[-2:]
        slot = plan_ref[ROUNDS - 1]
        copy_all(sems, [(came_ref.at[0], out.at[slot]), (kept_ref.at[0], out.at[1 - slot])])

    return copier(kernel, [(2,) + came.shape[1:]], 2, plan, came, kept, *held_back)[0]


def sum_kernel(*refs):
    out_ref = refs[-1]
    half = out_ref.shape[-1] // 2
    for chunk in range(CHUNKS):
        parts = refs[chunk * WINDOW : (chunk + 1) * WINDOW]
        for group in range(SHARE):
            for kind in range(2):
                at = (group * 2 + kind) * HEAD
                to = kind * half + (chunk * SHARE + group) * HEAD
                total = parts[0][:, :, at : at + HEAD].astype(jnp.float32)
                for part in parts[1:]:
                    total = total + part[:, :, at : at + HEAD].astype(jnp.float32)
                out_ref[:, :, to : to + HEAD] = total.astype(out_ref.dtype)


def sum_of(chunks, held_back=()):
    vmem = pl.BlockSpec(memory_space=pltpu.VMEM)
    rows, toks, cols = chunks[0][0].shape
    return pl.pallas_call(
        sum_kernel,
        in_specs=[vmem] * (WINDOW * CHUNKS) + [ANYWHERE] * len(held_back),
        out_specs=vmem,
        out_shape=jax.ShapeDtypeStruct((rows, toks, cols * CHUNKS), jnp.bfloat16),
        **light(4 * 1024 * 1024),
    )(*[part for parts in chunks for part in parts], *held_back)


def columns_kernel(count, place_ref, *refs):
    sources, outs = refs[: 4 * count], refs[-count:]
    part = sources[0].shape[1]
    for k, out in enumerate(outs):
        for side in range(2):
            for low in range(2):
                out[side, :, low * part : (low + 1) * part] = sources[(k * 2 + side) * 2 + low][...]


def columns_of(place, flat, chips, held_back=()):
    rows, width = flat.shape
    part = width // (2 * TEAM)
    in_specs = []
    for k in chips:
        for side in range(2):
            for low in range(2):
                in_specs.append(
                    pl.BlockSpec(
                        (rows, part),
                        lambda i, p, bits=2 * k + side, low=low: (0, low * TEAM + (p[0] ^ bits)),
                    )
                )
    shape = jax.ShapeDtypeStruct((2, rows, 2 * part), flat.dtype)
    out = pl.BlockSpec((2, rows, 2 * part), lambda i, p: (0, 0, 0))
    return pl.pallas_call(
        functools.partial(columns_kernel, len(chips)),
        grid_spec=pltpu.PrefetchScalarGridSpec(
            num_scalar_prefetch=1,
            grid=(1,),
            in_specs=in_specs + [ANYWHERE] * len(held_back),
            out_specs=[out] * len(chips),
        ),
        out_shape=[shape] * len(chips),
        **light(1024 * 1024),
    )(place, *([flat] * len(in_specs)), *held_back)


def hold_kernel(*refs):
    pass


def hold(array, *held_back):
    return pl.pallas_call(
        hold_kernel,
        in_specs=[ANYWHERE] * (1 + len(held_back)),
        out_specs=ANYWHERE,
        out_shape=jax.ShapeDtypeStruct(array.shape, array.dtype),
        input_output_aliases={0: 0},
        **light(1024),
    )(array, *held_back)


def attention_kernel(info_ref, *refs):
    q_ref, d_ref = refs[:2]
    k_refs = refs[2 : 2 + WINDOW]
    v_refs = refs[2 + WINDOW : 2 + 2 * WINDOW]
    start_ref = refs[2 + 2 * WINDOW]
    outs = len(refs) - 7 - WINDOW
    dq_ref = refs[outs]
    part_refs = refs[outs + 1 : outs + 1 + WINDOW]
    q_s, d_s, w_s, dp_s, acc_s, sum_s = refs[-6:]
    first = info_ref[1]
    heads = q_ref.shape[-1] // HEAD
    scale = HEAD ** (-0.5)
    for head in range(heads):
        at = slice(head * HEAD, (head + 1) * HEAD)
        q_s[head * BLOCK : (head + 1) * BLOCK, :] = q_ref[0, :, at]
        d_s[head * BLOCK : (head + 1) * BLOCK, :] = d_ref[0, :, at]
    start = start_ref[0]
    key_iota = lax.broadcasted_iota(jnp.int32, (JOIN * BLOCK, BLOCK), 0)
    query_iota = lax.broadcasted_iota(jnp.int32, (JOIN * BLOCK, BLOCK), 1) + (WINDOW - 1) * BLOCK
    sum_s[...] = jnp.zeros_like(sum_s)
    acc_s[...] = jnp.zeros_like(acc_s)
    span = 2 * BLOCK
    spans = [slice(at, at + span) for at in range(0, heads * BLOCK, span)]

    def fold(array):
        return jnp.sum(array.reshape(JOIN * BLOCK // 8, 8, span), axis=0)

    for index in range(0, WINDOW, JOIN):
        at = slice(index * BLOCK, (index + JOIN) * BLOCK)

        @pl.when(index + JOIN > first)
        def _():
            key_pos = key_iota + index * BLOCK
            seen = (key_pos >= start) & (key_pos <= query_iota)
            bias = jnp.where(seen, 0.0, MASKED)
            bias = jnp.concatenate([bias, bias], axis=1)
            key = jnp.concatenate([k_refs[index + i][0] for i in range(JOIN)], axis=0)
            value = jnp.concatenate([v_refs[index + i][0] for i in range(JOIN)], axis=0)
            for cols in spans:
                scores = lax.dot_general(key, q_s[cols, :], NT, preferred_element_type=jnp.float32)
                dprobs = lax.dot_general(
                    value, d_s[cols, :], NT, preferred_element_type=jnp.float32
                )
                weights = jnp.exp2(scores * (scale * LOG2E) + bias)
                w_s[at, cols] = weights
                dp_s[at, cols] = dprobs
                sum_s[0:8, cols] += fold(weights)
                sum_s[8:16, cols] += fold(weights * dprobs)

    inverse = 1.0 / jnp.sum(sum_s[0:8, :], axis=0, keepdims=True)
    delta = jnp.sum(sum_s[8:16, :], axis=0, keepdims=True) * inverse

    for index in range(0, WINDOW, JOIN):
        at = slice(index * BLOCK, (index + JOIN) * BLOCK)
        joined = range(index, index + JOIN)

        @pl.when(index + JOIN <= first)
        def _():
            for i in joined:
                part_refs[i][0] = jnp.zeros(part_refs[i].shape[1:], jnp.bfloat16)

        @pl.when(index + JOIN > first)
        def _():
            key = [k_refs[i][0].astype(jnp.float32).T.astype(jnp.bfloat16) for i in joined]
            key = jnp.concatenate(key, axis=1)
            dk = jnp.zeros((JOIN * BLOCK, HEAD), jnp.float32)
            dv = jnp.zeros((JOIN * BLOCK, HEAD), jnp.float32)
            for cols in spans:
                probs = w_s[at, cols] * inverse[:, cols]
                dscores = (probs * (dp_s[at, cols] - delta[:, cols]) * scale).astype(jnp.bfloat16)
                dv += jnp.dot(
                    probs.astype(jnp.bfloat16), d_s[cols, :], preferred_element_type=jnp.float32
                )
                dk += jnp.dot(dscores, q_s[cols, :], preferred_element_type=jnp.float32)
                acc_s[:, cols] += jnp.dot(key, dscores, preferred_element_type=jnp.float32)
            for i in joined:
                rows = slice((i - index) * BLOCK, (i - index + 1) * BLOCK)
                part_refs[i][0, :, :HEAD] = dk[rows].astype(jnp.bfloat16)
                part_refs[i][0, :, HEAD:] = dv[rows].astype(jnp.bfloat16)

    for head in range(heads):
        at = slice(head * HEAD, (head + 1) * HEAD)
        dq_ref[0, :, at] = acc_s[:, head * BLOCK : (head + 1) * BLOCK].T.astype(jnp.bfloat16)


def attention(info, page, blocks, start, chunk, dq, parts, held_back=(), dq_width=4096):
    _, toks, page_width = page.shape
    rows = start.shape[0]
    width = dq_width // GROUPS
    first = chunk * SHARE if page_width == dq_width else 0
    queries = width // HEAD * toks
    pairs = SHARE * queries * WINDOW * BLOCK
    in_specs = [
        pl.BlockSpec((1, toks, width), lambda g, f: (0, 0, first + g)),
        pl.BlockSpec((1, toks, width), lambda g, f: (1, 0, first + g)),
    ]
    in_specs += [pl.BlockSpec((1, BLOCK, HEAD), lambda g, f: (f[0], 0, chunk * SHARE + g))] * WINDOW
    in_specs += [
        pl.BlockSpec((1, BLOCK, HEAD), lambda g, f: (f[0], 0, GROUPS + chunk * SHARE + g))
    ] * WINDOW
    in_specs += [pl.BlockSpec((1, 1, toks), lambda g, f: (f[0], 0, 0))]
    args = [page, page] + list(blocks) + list(blocks) + [start]
    aliases = {}
    for place, array in enumerate([dq] + list(parts)):
        if array is not None:
            aliases[1 + len(args)] = place
            in_specs.append(ANYWHERE)
            args.append(array)
    in_specs += [ANYWHERE] * len(held_back)
    args += held_back
    part_shape = jax.ShapeDtypeStruct((rows, BLOCK, SHARE * 2 * HEAD), jnp.bfloat16)
    spec = pltpu.PrefetchScalarGridSpec(
        num_scalar_prefetch=1,
        grid=(SHARE,),
        in_specs=in_specs,
        out_specs=[pl.BlockSpec((1, toks, width), lambda g, f: (f[0], 0, chunk * SHARE + g))]
        + [pl.BlockSpec((1, BLOCK, 2 * HEAD), lambda g, f: (f[0], 0, g))] * WINDOW,
        scratch_shapes=[
            pltpu.VMEM((queries, HEAD), jnp.bfloat16),
            pltpu.VMEM((queries, HEAD), jnp.bfloat16),
            pltpu.VMEM((WINDOW * BLOCK, queries), jnp.float32),
            pltpu.VMEM((WINDOW * BLOCK, queries), jnp.float32),
            pltpu.VMEM((HEAD, queries), jnp.float32),
            pltpu.VMEM((16, queries), jnp.float32),
        ],
    )
    return pl.pallas_call(
        attention_kernel,
        grid_spec=spec,
        out_shape=[jax.ShapeDtypeStruct((rows, toks, GROUPS * width), jnp.bfloat16)]
        + [part_shape] * WINDOW,
        input_output_aliases=aliases,
        compiler_params=pltpu.CompilerParams(vmem_limit_bytes=VMEM),
        cost_estimate=pl.CostEstimate(
            flops=10 * pairs * HEAD, bytes_accessed=4 * 1024 * 1024, transcendentals=pairs
        ),
    )(info, *args)


def arrange_kernel(plan_ref, place_ref, *refs):
    sources, out_ref = refs[:-1], refs[-1]
    rank_me, z_me, low_me, high_me = (place_ref[i] for i in range(4))
    for rel, source in enumerate(sources):
        for page in range(2):
            rank = rank_me ^ rel
            slot = jnp.int32(page)
            for step in range(ROUNDS):
                to_rank = rank ^ (1 << step)
                goes = plan_ref[(rank ^ rank_me) * ROUNDS + step] == slot
                slot = jnp.where(goes, plan_ref[(to_rank ^ rank_me) * ROUNDS + step], slot)
                rank = jnp.where(goes, to_rank, rank)
            column = pl.multiple_of(((rank ^ rank_me) * 2 + slot) * BLOCK, BLOCK)
            data = source[page * BLOCK : (page + 1) * BLOCK, :].astype(jnp.float32)
            data = data.T.astype(jnp.bfloat16)
            for low in range(2):
                for high in range(2):
                    for z in range(4):
                        at = ((low * 2 + high) * 4 + z) * 32
                        to = (z ^ z_me) * 4 + (low ^ low_me) + (high ^ high_me) * 2
                        to = pl.multiple_of(to * 32, 32)
                        out_ref[pl.ds(to, 32), pl.ds(column, BLOCK)] = data[at : at + 32, :]


def arrange(plan_all, place, sources):
    rows, cols = sources[0].shape
    return pl.pallas_call(
        arrange_kernel,
        grid_spec=pltpu.PrefetchScalarGridSpec(
            num_scalar_prefetch=2,
            grid=(1,),
            in_specs=[pl.BlockSpec((rows, cols), lambda i, a, b: (0, 0))] * len(sources),
            out_specs=pl.BlockSpec((cols, rows * len(sources)), lambda i, a, b: (0, 0)),
        ),
        out_shape=jax.ShapeDtypeStruct((cols, rows * len(sources)), jnp.bfloat16),
        compiler_params=pltpu.CompilerParams(vmem_limit_bytes=VMEM),
        cost_estimate=pl.CostEstimate(flops=0, bytes_accessed=4 * 1024 * 1024, transcendentals=0),
    )(plan_all, place, *sources)


def product_kernel(x_ref, *refs):
    grads, outs = refs[:TEAM], refs[TEAM:]
    rows = jnp.concatenate([grad[slot] for grad in grads for slot in range(2)], axis=0)
    total = jnp.dot(x_ref[...], rows, preferred_element_type=jnp.float32)
    for z, out in enumerate(outs):
        out[...] = total[z * 4 * 32 : (z + 1) * 4 * 32].astype(out.dtype)


def product(x, grads):
    cols = grads[0].shape[-1]
    shape = (x.shape[0] // 4, cols)
    return pl.pallas_call(
        product_kernel,
        out_shape=[jax.ShapeDtypeStruct(shape, jnp.float32)]
        + [jax.ShapeDtypeStruct(shape, jnp.bfloat16)] * 3,
        compiler_params=pltpu.CompilerParams(vmem_limit_bytes=VMEM),
        cost_estimate=pl.CostEstimate(
            flops=2 * x.shape[0] * x.shape[1] * cols,
            bytes_accessed=5 * 1024 * 1024,
            transcendentals=0,
        ),
    )(x, *grads)


def per_device(tokens, queries, out_grad, kv_weight, doc_lengths, swap_plan):
    seqs, toks, width = tokens.shape
    pair = kv_weight.shape[1]
    cols = pair // 2
    group_width = queries.shape[2] // GROUPS
    dp = lax.axis_index("dp")
    ctx = lax.axis_index("ctx")
    rank = lax.rem(dp, TEAM)
    z = lax.rem(ctx, 4)
    y_high = ctx // 4
    y_low = dp // TEAM
    plan = swap_plan[0, 0]
    plans = jnp.stack([plan] + [move(plan, flip_dp(2 * k)) for k in range(1, TEAM // 2)])
    plan_all = jnp.stack([plans, move(plans, flip_dp(1))], axis=1).reshape(-1)

    ends = jnp.cumsum(doc_lengths, axis=1)
    pos = ctx * toks + jnp.arange(toks, dtype=jnp.int32)
    begun = jnp.max(
        jnp.where(ends[:, None, :] <= pos[None, :, None], ends[:, None, :], 0), axis=2
    )
    start = begun - (ctx - (WINDOW - 1)) * toks
    first = jnp.clip(start[:, 0] // BLOCK, 0, WINDOW - 1)
    start = start[:, None, :]
    row_came = plan[ROUNDS - 1]
    row_kept = 1 - row_came
    info_came = jnp.stack([row_came, jnp.where(row_came == 0, first[0], first[1])])
    info_kept = jnp.stack([row_kept, jnp.where(row_kept == 0, first[0], first[1])])

    def cross(step, value):
        return move(value, flip_dp(1 << step))

    halves = [queries, out_grad]
    flat = tokens.reshape(seqs * toks, width)
    kv = jnp.dot(flat, kv_weight, preferred_element_type=jnp.float32).astype(jnp.bfloat16)
    kv = kv.reshape(seqs, toks, pair)
    kv_came = cross(0, pages_of(plan, [kv], [plan_all])[0])
    send = second_pages_of(plan, [kv_came], [kv])
    loaded = [cross(0, one) for one in pages_of(plan, halves, [send])]
    kv_second = cross(1, send)
    send, kv_kept = third_pages_of(plan, kv_second, [kv_came], [kv], 0, 1, True)
    kv_third = cross(2, send)
    send = second_pages_of(plan, loaded, halves)
    send = hold(send, kv_third)
    came = cross(1, send)
    own = rows_of(plan, kv_third, kv_kept, [send])
    near = [move(own, shift_z(by)) for by in (1, 2, 3)]
    above = move(own, lift)
    far = [
        move(above, shift_z(1, {(1, 0), (1, 1), (1, 2), (1, 3)}, True)),
        move(above, shift_z(2, {(1, 2), (1, 3)}, True)),
        move(above, shift_z(3, {(1, 1), (1, 2), (1, 3)}, True)),
    ]
    blocks = [
        far[0],
        above,
        near[2] + far[2],
        near[1] + far[1],
        jnp.where(z == 0, far[0], near[0]),
        own,
    ]
    send_a, kept = third_pages_of(
        plan, came, loaded, halves, 0, CHUNKS, True, held_back=near + far
    )
    came_a = cross(2, send_a)
    none = [None] * WINDOW

    def collect(parts):
        return parts[-1:] + [
            move(parts[WINDOW - 1 - by], shift_ctx(-by)) for by in range(1, WINDOW)
        ]

    there = [None] * (TEAM // 2)
    there[0], column = columns_of(rank[None], flat, [0, 2], [send_a])
    there[2] = move(column, flip_dp(4))
    dq, *parts_a = attention(info_kept, kept, blocks, start, 0, None, none)
    dq, *parts_b = attention(info_kept, kept, blocks, start, 1, dq, none)
    send_b = third_pages_of(
        plan, came, loaded, halves, 1, CHUNKS, False, held_back=[came_a, parts_b[0], there[2]]
    )[0]
    came_b = cross(2, send_b)
    dq, *parts_a = attention(info_came, came_a, blocks, start, 0, dq, parts_a)
    parts_a = collect(parts_a)
    columns = list(columns_of(rank[None], flat, [1, 3], [came_b]))
    for k, column in zip((1, 3), columns):
        there[k] = move(column, flip_dp(2 * k))
    dq, *parts_b = attention(
        info_came, came_b, blocks, start, 1, dq, parts_b, parts_a[1:4] + columns[:1]
    )
    grad = sum_of([parts_a, collect(parts_b)], [there[1], there[3]])

    sources = []
    for k in range(TEAM // 2):
        sources += [there[k][0], move(there[k][1], flip_dp(1))]
    place = jnp.stack([rank, z, y_low, y_high])
    arranged = arrange(plan_all, place, sources)
    grads = []
    for k in range(TEAM // 2):
        chip = move(grad, flip_dp(2 * k)) if k else grad
        grads += [chip, move(chip, flip_dp(1))]
    mine, *others = product(arranged, grads)
    for k, other in enumerate(others):
        mine = mine + move(other, flip_ctx(k + 1)).astype(jnp.float32)
    final = mine[:32]
    for k in range(1, 4):
        final = final + move(mine[32 * k : 32 * (k + 1)], flip_y(k % 2, k // 2))
    return dq, final


def solution(mesh):
    in_specs = (
        P("dp", "ctx", None),
        P("dp", "ctx", None),
        P("dp", "ctx", None),
        P(),
        P("dp", None),
        P("dp", "ctx", None),
    )
    out_specs = (P("dp", "ctx", None), P(("dp", "ctx"), None))
    return jax.shard_map(
        per_device, mesh=mesh, in_specs=in_specs, out_specs=out_specs, check_vma=False
    )
```
